32 devices in a mesh: ctx: 16 (over z, y, x), fsdp: 2 (over core).
Axes of the slice: x: 2, y: 2, z: 4, core: 2. Of those that a mesh axis runs over, the one named last changes fastest.
Arguments:
- query_rows: bfloat16 [4096, 4096], P(('ctx', 'fsdp')), may hold values from -40 to 40
- key_rows: bfloat16 [4096, 512], P(('ctx', 'fsdp')), may hold values from -6 to 6
- value_matrix: bfloat16 [4096, 512], P(('ctx', 'fsdp')), may hold values from -6 to 6
- out_grad: bfloat16 [4096, 4096], P(('ctx', 'fsdp')), may hold values from -24 to 24
- segments: int32 [4096], P(('ctx', 'fsdp')), may hold values from 0 to 4, never falling along the last dimension, each value on 1 to 1536 neighbouring positions
Outputs:
- query_grad: bfloat16 [4096, 4096], P(('ctx', 'fsdp'))
- key_grad: bfloat16 [4096, 512], P(('ctx', 'fsdp'))
- value_grad: bfloat16 [4096, 512], P(('ctx', 'fsdp'))
The draws below stay inside these ranges and needn't reach their ends.
Inputs may be any that keep to these rules, and one draw needn't show every extreme that they name: `segments`: segment numbers never fall along the sequence.
All inputs are finite; a program needn't handle non-finite values.
Results may differ from the reference program's by a relative error of at most 0.0085.
Values may be sent and summed in bfloat16 or wider, within the bound.
A program may use at most 64 MiB of HBM per device.

```python
import math
import jax
import jax.numpy as jnp
import numpy as np
from jax import lax

HEAD_WIDTH = 128
QUERY_HEADS = 32
KEY_VALUE_HEADS = 4
TOK_DEV = 128
WIN = 384
TOKEN_COUNT = 4096


def starting_keys(key):
    sender_index = jax.random.fold_in(key, 101)
    unscaled_input = jnp.clip(jax.random.normal(sender_index, (TOKEN_COUNT, KEY_VALUE_HEADS * HEAD_WIDTH), jnp.float32), -5.0, 5.0)
    return unscaled_input


def draw_key_rows(key, part):
    return starting_keys(key).astype(jnp.bfloat16)


def draw_query_rows(key, part):
    sender_index = jax.random.fold_in(key, 202)
    unscaled_input = jnp.clip(jax.random.normal(sender_index, (TOKEN_COUNT, QUERY_HEADS * HEAD_WIDTH), jnp.float32), -5.0, 5.0)
    return unscaled_input.astype(jnp.bfloat16)


def block_scale(key, dims, cuts, low, largest):
    def one(position, blocks):
        steps = jax.random.uniform(jax.random.fold_in(jax.random.fold_in(key, 6), position), (blocks,), jnp.float32, low / len(cuts), largest / len(cuts))
        return jnp.repeat(jnp.exp(steps), dims[position] // blocks).reshape((-1,) + (1,) * (len(dims) - position - 1))

    factor_of = one(*cuts[0])
    for cut in cuts[1:]:
        factor_of = factor_of * one(*cut)
    return factor_of


def split_up(count, total, limit, lean):
    loads = [(1 << 20) // math.isqrt(rank ** lean) + 1 for rank in range(2, count + 1)]
    rest, holding = total - limit - (count - 1), [1] * (count - 1)
    while rest > 0:
        movable = [i for i in range(count - 1) if holding[i] < limit]
        mass, left = sum([loads[i] for i in movable]), rest
        for i in movable:
            more = min(limit - holding[i], max(1, left * loads[i] // mass), rest)
            holding[i] = holding[i] + more
            rest = rest - more
    return np.array([limit] + holding)


def uneven(key, count, total, limit, slope):
    if count == 2:
        one = jax.random.randint(key, (), max(1, total - limit), min(limit, total - 1) + 1)
        return jnp.stack([one, total - one])
    tallies = jnp.asarray(split_up(count, total, limit, slope), jnp.int32)
    pairs = (count - 1) // 2
    source_of, receiver = tallies[1:1 + 2 * pairs:2], tallies[2:2 + 2 * pairs:2]
    room = jnp.minimum(source_of - 1, limit - receiver)
    moved = jax.random.randint(jax.random.fold_in(key, 1), (pairs,), 0, 1 << 20) % (room + 1)
    tallies = tallies.at[1:1 + 2 * pairs:2].set(source_of - moved).at[2:2 + 2 * pairs:2].set(receiver + moved)
    return tallies[jax.random.permutation(jax.random.fold_in(key, 2), count)]


def bell_draw(stream_key, extent, width, reach, split=(), kind=jnp.bfloat16):
    entries = jax.random.normal(stream_key, extent, jnp.float32) * width
    if len(split) > 0:
        entries = block_scale(stream_key, extent, split, -0.22, 0.18) * entries
    return jnp.clip(entries, min=-reach, max=reach).astype(kind)


def setup_inputs(seed: int = 0) -> dict:
    arg_keys = jax.random.split(jax.random.key(seed), 6)
    return {
        "query_rows": draw_query_rows(jax.random.fold_in(arg_keys[5], 71), 0),
        "key_rows": draw_key_rows(jax.random.fold_in(arg_keys[5], 71), 0),
        "value_matrix": bell_draw(arg_keys[2], (TOKEN_COUNT, KEY_VALUE_HEADS * HEAD_WIDTH), 1.0, 6.0, ((0, 32),)),
        "out_grad": bell_draw(arg_keys[3], (TOKEN_COUNT, QUERY_HEADS * HEAD_WIDTH), 4.0, 24.0, ((0, 32),)),
        "segments": jnp.searchsorted(jnp.cumsum(uneven(arg_keys[4], TOKEN_COUNT // (2 * WIN), TOKEN_COUNT, 4 * WIN, 2)), jnp.arange(TOKEN_COUNT), side="right").astype(jnp.int32),
    }


def band_grads(query_blk, grad_blk, key_win, value_win, query_seg, key_seg, query_first, key_first, window):
    tok_rows = query_blk.shape[0]
    key_count = key_win.shape[0]
    kv_heads = key_win.shape[1] // HEAD_WIDTH
    heads_per_group = query_blk.shape[1] // key_win.shape[1]
    inv_root = 1.0 / math.sqrt(HEAD_WIDTH)
    query_pos = query_first + jnp.arange(tok_rows, dtype=jnp.int32)
    key_pos = key_first + jnp.arange(key_count, dtype=jnp.int32)
    allowed = (key_pos[None, :] > query_pos[:, None] - window) & (key_pos[None, :] <= query_pos[:, None])
    allowed = allowed & (key_pos[None, :] >= 0) & (key_seg[None, :] == query_seg[:, None])
    query_parts = []
    key_parts = []
    value_parts = []
    for kv_head in range(kv_heads):
        k_head = key_win[:, kv_head * HEAD_WIDTH:(kv_head + 1) * HEAD_WIDTH].astype(jnp.float32)
        v_head = value_win[:, kv_head * HEAD_WIDTH:(kv_head + 1) * HEAD_WIDTH].astype(jnp.float32)
        lower = kv_head * heads_per_group * HEAD_WIDTH
        q_head = query_blk[:, lower:lower + heads_per_group * HEAD_WIDTH].reshape(tok_rows, heads_per_group, HEAD_WIDTH).astype(jnp.float32)
        o_grad = grad_blk[:, lower:lower + heads_per_group * HEAD_WIDTH].reshape(tok_rows, heads_per_group, HEAD_WIDTH).astype(jnp.float32)
        scores = jnp.einsum('trd,kd->rtk', q_head, k_head) * inv_root
        scores = jnp.where(allowed[None], scores, -1e+30)
        row_max = lax.optimization_barrier(jnp.max(scores, axis=-1, keepdims=True))
        weights = jnp.exp(scores - row_max)
        probs = weights / lax.optimization_barrier(jnp.sum(weights, axis=-1, keepdims=True))
        prob_grad = jnp.einsum('trd,kd->rtk', o_grad, v_head)
        row_delta = lax.optimization_barrier(jnp.sum(probs * prob_grad, axis=-1, keepdims=True))
        score_grad = lax.optimization_barrier((probs * (prob_grad - row_delta) * inv_root).astype(jnp.bfloat16)).astype(jnp.float32)
        probs_low = lax.optimization_barrier(probs.astype(jnp.bfloat16)).astype(jnp.float32)
        query_parts.append(jnp.einsum('rtk,kd->trd', score_grad, k_head).reshape(tok_rows, heads_per_group * HEAD_WIDTH))
        key_parts.append(jnp.einsum('rtk,trd->kd', score_grad, q_head))
        value_parts.append(jnp.einsum('rtk,trd->kd', probs_low, o_grad))
    return (jnp.concatenate(query_parts, 1), jnp.concatenate(key_parts, 1), jnp.concatenate(value_parts, 1))

def reference(query_rows, key_rows, value_matrix, out_grad, segments):
    block_count = TOKEN_COUNT // TOK_DEV
    key_count = WIN + TOK_DEV
    kv_width = key_rows.shape[1]
    key_padded = jnp.concatenate([jnp.zeros((WIN, kv_width), key_rows.dtype), key_rows], 0)
    value_padded = jnp.concatenate([jnp.zeros((WIN, kv_width), value_matrix.dtype), value_matrix], 0)
    seg_padded = jnp.concatenate([-jnp.ones((WIN,), jnp.int32), segments.astype(jnp.int32)], 0)

    def advance(carry, block_index):
        key_acc, value_acc = carry
        query_first = (block_index * TOK_DEV).astype(jnp.int32)
        query_blk = lax.dynamic_slice_in_dim(query_rows, query_first, TOK_DEV, 0)
        grad_blk = lax.dynamic_slice_in_dim(out_grad, query_first, TOK_DEV, 0)
        query_seg = lax.dynamic_slice_in_dim(segments.astype(jnp.int32), query_first, TOK_DEV, 0)
        key_win = lax.dynamic_slice_in_dim(key_padded, query_first, key_count, 0)
        value_win = lax.dynamic_slice_in_dim(value_padded, query_first, key_count, 0)
        key_seg = lax.dynamic_slice_in_dim(seg_padded, query_first, key_count, 0)
        dq_part, dk_part, dv_part = band_grads(query_blk, grad_blk, key_win, value_win, query_seg, key_seg, query_first, query_first - WIN, WIN)
        key_acc = lax.dynamic_update_slice_in_dim(key_acc, lax.dynamic_slice_in_dim(key_acc, query_first, key_count, 0) + dk_part, query_first, 0)
        value_acc = lax.dynamic_update_slice_in_dim(value_acc, lax.dynamic_slice_in_dim(value_acc, query_first, key_count, 0) + dv_part, query_first, 0)
        return ((key_acc, value_acc), dq_part.astype(jnp.bfloat16))
    zeros = jnp.zeros((TOKEN_COUNT + WIN, kv_width), jnp.float32)
    (key_acc, value_acc), dq_blocks = lax.scan(advance, (zeros, zeros), jnp.arange(block_count, dtype=jnp.int32))
    query_grad = dq_blocks.reshape(TOKEN_COUNT, dq_blocks.shape[2])
    return (query_grad, key_acc[WIN:].astype(jnp.bfloat16), value_acc[WIN:].astype(jnp.bfloat16))
```

```python
import functools
import math

import jax
import jax.numpy as jnp
from jax import lax
from jax.experimental import pallas as pl
from jax.experimental.pallas import tpu as pltpu
from jax.sharding import PartitionSpec as P

HEAD = 128
GROUP = 8
TOK = 128
SLOTS = 5
WIDE = GROUP * HEAD
INV_ROOT = 1.0 / math.sqrt(HEAD)
TO_EXP2 = INV_ROOT * math.log2(math.e)
MESH = pl.DeviceIdType.MESH
NT = (((1,), (1,)), ((), ()))


def kernel(
    inner, count,
    q_in, k_in, v_in, o_in, seg_in,
    dq_out, dk_out, dv_out,
    qb, ob, kw, vw, segw, bias, pb, sb, dqs, acc_k, acc_v, stage, back,
    local_sem, seg_send, seg_recv, kv_send, kv_recv, q_send, q_recv,
    dq_sem, dq_recv, back_send, back_recv,
):
    pos = lax.axis_index("ctx") * inner + lax.axis_index("fsdp")
    pairs = count // 2
    pair, core = pos // 2, pos % 2
    other = 1 - core

    def place(p):
        return (p // inner, p % inner)

    partner = 2 * pair + other
    has_next = pair + 1 < pairs
    has_next2 = jnp.logical_and(core == 1, pair + 2 < pairs)
    has_prev = pair >= 1
    has_prev2 = pair >= 2

    def kv_cols(h):
        return pl.ds(pl.multiple_of(h * HEAD, HEAD), HEAD)

    def q_cols(h):
        return pl.ds(pl.multiple_of(h * WIDE, WIDE), WIDE)

    own = []
    for gl in range(2):
        h = 2 * core + gl
        own.append(
            (
                pltpu.make_async_copy(k_in.at[:, kv_cols(h)], kw.at[gl, 3 + core], local_sem.at[0, gl]),
                pltpu.make_async_copy(v_in.at[:, kv_cols(h)], vw.at[gl, 3 + core], local_sem.at[1, gl]),
                pltpu.make_async_copy(q_in.at[:, q_cols(h)], qb.at[gl, core], local_sem.at[2, gl]),
                pltpu.make_async_copy(o_in.at[:, q_cols(h)], ob.at[gl, core], local_sem.at[3, gl]),
            )
        )

    barrier = pltpu.get_barrier_semaphore()

    def greet(p):
        pl.semaphore_signal(barrier, inc=1, device_id=place(p), device_id_type=MESH)

    greet(partner)

    @pl.when(has_next)
    def _():
        greet(2 * pair + 2)
        greet(2 * pair + 3)

    @pl.when(has_prev)
    def _():
        greet(2 * pair - 2)
        greet(2 * pair - 1)

    @pl.when(has_next2)
    def _():
        greet(2 * pair + 4)
        greet(2 * pair + 5)

    @pl.when(has_prev2)
    def _():
        greet(2 * pair - 3)

    for gl in range(2):
        for copy in own[gl]:
            copy.start()

    segw[3 + core] = jnp.broadcast_to(seg_in[...], (8, TOK))

    @pl.when(jnp.logical_not(has_prev2))
    def _():
        for gl in range(2):
            kw[gl, 0] = jnp.zeros((TOK, HEAD), jnp.bfloat16)
            vw[gl, 0] = jnp.zeros((TOK, HEAD), jnp.bfloat16)
        segw[0] = jnp.full((8, TOK), -1, jnp.int32)

    @pl.when(jnp.logical_not(has_prev))
    def _():
        for slot in (1, 2):
            for gl in range(2):
                kw[gl, slot] = jnp.zeros((TOK, HEAD), jnp.bfloat16)
                vw[gl, slot] = jnp.zeros((TOK, HEAD), jnp.bfloat16)
            segw[slot] = jnp.full((8, TOK), -1, jnp.int32)

    @pl.when(jnp.logical_not(has_next))
    def _():
        back[:, :, 0:2] = jnp.zeros((2, 2, 2, TOK, HEAD), jnp.bfloat16)

    @pl.when(jnp.logical_not(has_next2))
    def _():
        back[:, :, 2:4] = jnp.zeros((2, 2, 2, TOK, HEAD), jnp.bfloat16)

    signals = (
        1 + 2 * has_next.astype(jnp.int32) + 2 * has_prev.astype(jnp.int32)
        + 2 * has_next2.astype(jnp.int32) + has_prev2.astype(jnp.int32)
    )
    pl.semaphore_wait(barrier, signals)

    targets = [
        (0, 2 * pair + 2, has_next, 1 + core, 0),
        (1, 2 * pair + 3, has_next, 1 + core, 2),
        (2, 2 * pair + 4, has_next2, 0, 0),
        (3, 2 * pair + 5, has_next2, 0, 2),
        (4, partner, None, 3 + core, 2 * other),
    ]

    def guarded(cond, fn):
        if cond is None:
            fn()
        else:
            pl.when(cond)(fn)

    def seg_copy(target):
        n, p, _, slot, _ = target
        return pltpu.make_async_remote_copy(
            segw.at[3 + core], segw.at[slot], seg_send.at[n], seg_recv.at[slot], place(p), MESH
        )

    def kv_copies(target, gl):
        n, p, _, slot, head = target
        cols = kv_cols(head + gl)
        return (
            pltpu.make_async_remote_copy(
                k_in.at[:, cols], kw.at[gl, slot], kv_send.at[0, gl, n], kv_recv.at[0, gl, slot], place(p), MESH
            ),
            pltpu.make_async_remote_copy(
                v_in.at[:, cols], vw.at[gl, slot], kv_send.at[1, gl, n], kv_recv.at[1, gl, slot], place(p), MESH
            ),
        )

    def q_copies(gl):
        cols = q_cols(2 * other + gl)
        return (
            pltpu.make_async_remote_copy(
                q_in.at[:, cols], qb.at[gl, core], q_send.at[0, gl], q_recv.at[0, gl], place(partner), MESH
            ),
            pltpu.make_async_remote_copy(
                o_in.at[:, cols], ob.at[gl, core], q_send.at[1, gl], q_recv.at[1, gl], place(partner), MESH
            ),
        )

    for target in targets:
        def start_seg(target=target):
            seg_copy(target).start()
        guarded(target[2], start_seg)
    for gl in range(2):
        for target in targets:
            def start_kv(target=target, gl=gl):
                for copy in kv_copies(target, gl):
                    copy.start()
            guarded(target[2], start_kv)
        for copy in q_copies(gl):
            copy.start()

    def landed(ref, sem):
        pltpu.make_async_remote_copy(ref, ref, sem, sem, place(partner), MESH).wait_recv()

    def each_arrival(fn):
        guarded(has_prev2, lambda: fn(0))

        def near():
            fn(1)
            fn(2)
        guarded(has_prev, near)
        fn(3 + other)

    each_arrival(lambda slot: landed(segw.at[slot], seg_recv.at[slot]))
    row = lax.broadcasted_iota(jnp.int32, (TOK, TOK), 0)
    col = lax.broadcasted_iota(jnp.int32, (TOK, TOK), 1)
    key_seg = [
        jnp.broadcast_to(segw[slot, 0:1, :].astype(jnp.float32), (TOK, TOK)).T for slot in range(SLOTS)
    ]
    for t in range(2):
        query_seg = segw[3 + t, 0:1, :].astype(jnp.float32)
        for b in range(4):
            ok = key_seg[t + b] == query_seg
            if b == 0:
                ok = jnp.logical_and(ok, row > col)
            if b == 3:
                ok = jnp.logical_and(ok, row <= col)
            bias[t, b] = jnp.where(ok, 0.0, -1e30)

    def kv_wait(gl):
        own[gl][0].wait()
        own[gl][1].wait()

        def one(slot):
            landed(kw.at[gl, slot], kv_recv.at[0, gl, slot])
            landed(vw.at[gl, slot], kv_recv.at[1, gl, slot])
        each_arrival(one)

    def q_wait(gl):
        own[gl][2].wait()
        own[gl][3].wait()
        landed(qb.at[gl, other], q_recv.at[0, gl])
        landed(ob.at[gl, other], q_recv.at[1, gl])

    def stacked(block):
        heads = block.shape[1] // HEAD
        return jnp.concatenate([block[:, i * HEAD : (i + 1) * HEAD] for i in range(heads)], 0)

    def dq_copies(gl, t):
        cols = q_cols(2 * core + gl)
        return (
            pltpu.make_async_copy(dqs.at[gl, t], dq_out.at[:, cols], dq_sem.at[gl, 0]),
            pltpu.make_async_remote_copy(
                dqs.at[gl, t], dq_out.at[:, cols], dq_sem.at[gl, 1], dq_recv.at[gl], place(partner), MESH
            ),
        )

    def unit(gl, t, first):
        keys = kw[gl, t : t + 4].reshape(4 * TOK, HEAD)
        vals = vw[gl, t : t + 4].reshape(4 * TOK, HEAD)
        keys_t = keys.astype(jnp.float32).T.astype(jnp.bfloat16)

        def step(hp, carry):
            cols = pl.ds(pl.multiple_of(hp * 2 * HEAD, 2 * HEAD), 2 * HEAD)
            q = stacked(qb[gl, t, :, cols])
            o = stacked(ob[gl, t, :, cols])
            mask = bias[t].reshape(4 * TOK, TOK)
            mask = jnp.concatenate([mask, mask], 1)
            s = lax.dot_general(keys, q, NT, preferred_element_type=jnp.float32) * TO_EXP2 + mask
            dp = lax.dot_general(vals, o, NT, preferred_element_type=jnp.float32)
            top = jnp.max(s, axis=0, keepdims=True)
            w = jnp.exp2(s - top)
            r = 1.0 / jnp.sum(w, axis=0, keepdims=True)
            delta = jnp.sum(w * dp, axis=0, keepdims=True) * r
            probs = w * r
            ds = (probs * (dp - delta)).astype(jnp.bfloat16)
            pb[:, cols] = probs.astype(jnp.bfloat16)
            sb[:, cols] = ds
            dq = (jnp.dot(keys_t, ds, preferred_element_type=jnp.float32) * INV_ROOT).T
            dqs[gl, t, :, cols] = jnp.concatenate([dq[:TOK], dq[TOK:]], 1).astype(jnp.bfloat16)
            return carry

        lax.fori_loop(0, GROUP // 2, step, 0)

        def send_local():
            dq_copies(gl, t)[0].start()

        def send_remote():
            dq_copies(gl, t)[1].start()

        pl.when(core == t)(send_local)
        pl.when(core != t)(send_remote)
        dk = jnp.dot(sb[...], stacked(qb[gl, t]), preferred_element_type=jnp.float32) * INV_ROOT
        dv = jnp.dot(pb[...], stacked(ob[gl, t]), preferred_element_type=jnp.float32)
        dk = dk.reshape(4, TOK, HEAD)
        dv = dv.reshape(4, TOK, HEAD)
        for b in range(4):
            slot = t + b
            if first or slot == 0 or slot == 4:
                acc_k[gl, slot] = dk[b]
                acc_v[gl, slot] = dv[b]
            else:
                acc_k[gl, slot] += dk[b]
                acc_v[gl, slot] += dv[b]

    homes = [
        (0, 2 * pair - 3, has_prev2, 0, 2 + core),
        (1, 2 * pair - 2, has_prev, 1, core),
        (2, 2 * pair - 1, has_prev, 2, core),
        (3, partner, None, 3 + other, 4),
    ]

    def back_copies(home, gl):
        n, p, _, slot, spot = home
        return [
            pltpu.make_async_remote_copy(
                stage.at[i, gl, n], back.at[i, gl, spot], back_send.at[i, gl, n],
                back_recv.at[i, gl, spot], place(p), MESH,
            )
            for i in range(2)
        ]

    def send_back(gl, numbers):
        for n in numbers:
            home = homes[n]
            slot = home[3]
            stage[0, gl, n] = acc_k[gl, slot].astype(jnp.bfloat16)
            stage[1, gl, n] = acc_v[gl, slot].astype(jnp.bfloat16)

            def start(home=home):
                for copy in back_copies(home, gl):
                    copy.start()
            guarded(home[2], start)

    kv_wait(0)
    q_wait(0)
    unit(0, 1, True)
    unit(0, 0, False)
    send_back(0, (0, 1, 2, 3))
    kv_wait(1)
    q_wait(1)
    unit(1, 0, True)
    send_back(1, (0,))
    unit(1, 1, False)
    send_back(1, (1, 2, 3))

    for gl in range(2):
        def near(gl=gl):
            for i in range(2):
                for spot in (0, 1):
                    landed(back.at[i, gl, spot], back_recv.at[i, gl, spot])
        guarded(has_next, near)

        def far(gl=gl):
            for i in range(2):
                for spot in (2, 3):
                    landed(back.at[i, gl, spot], back_recv.at[i, gl, spot])
        guarded(has_next2, far)
        for i in range(2):
            landed(back.at[i, gl, 4], back_recv.at[i, gl, 4])
        for i, acc, out in ((0, acc_k, dk_out), (1, acc_v, dv_out)):
            mine = acc[gl, 3 + core]
            mine += back[i, gl, core].astype(jnp.float32)
            mine += back[i, gl, 2 + core].astype(jnp.float32)
            out[:, kv_cols(2 * core + gl)] = mine.astype(jnp.bfloat16)
            rest = back[i, gl, 4].astype(jnp.float32)
            rest += back[i, gl, other].astype(jnp.float32)
            rest += back[i, gl, 2 + other].astype(jnp.float32)
            out[:, kv_cols(2 * other + gl)] = rest.astype(jnp.bfloat16)

    for target in targets:
        def sent(target=target):
            seg_copy(target).wait_send()
            for gl in range(2):
                for copy in kv_copies(target, gl):
                    copy.wait_send()
        guarded(target[2], sent)
    for gl in range(2):
        for copy in q_copies(gl):
            copy.wait_send()
        for home in homes:
            def returned(home=home, gl=gl):
                for copy in back_copies(home, gl):
                    copy.wait_send()
            guarded(home[2], returned)
        dq_copies(gl, 0)[0].wait()
        dq_copies(gl, 0)[1].wait_send()
        landed(dq_out.at[:, q_cols(2 * other + gl)], dq_recv.at[gl])


def body(count, inner, query_rows, key_rows, value_matrix, out_grad, segments):
    bf16, f32 = jnp.bfloat16, jnp.float32
    dma = pltpu.SemaphoreType.DMA
    anywhere = pl.BlockSpec(memory_space=pl.ANY)
    vmem = pl.BlockSpec(memory_space=pltpu.VMEM)
    return pl.pallas_call(
        functools.partial(kernel, inner, count),
        out_shape=(
            jax.ShapeDtypeStruct(query_rows.shape, bf16),
            jax.ShapeDtypeStruct(key_rows.shape, bf16),
            jax.ShapeDtypeStruct(value_matrix.shape, bf16),
        ),
        in_specs=[anywhere] * 4 + [vmem],
        out_specs=(anywhere, vmem, vmem),
        scratch_shapes=[
            pltpu.VMEM((2, 2, TOK, WIDE), bf16),
            pltpu.VMEM((2, 2, TOK, WIDE), bf16),
            pltpu.VMEM((2, SLOTS, TOK, HEAD), bf16),
            pltpu.VMEM((2, SLOTS, TOK, HEAD), bf16),
            pltpu.VMEM((SLOTS, 8, TOK), jnp.int32),
            pltpu.VMEM((2, 4, TOK, TOK), f32),
            pltpu.VMEM((4 * TOK, WIDE), bf16),
            pltpu.VMEM((4 * TOK, WIDE), bf16),
            pltpu.VMEM((2, 2, TOK, WIDE), bf16),
            pltpu.VMEM((2, SLOTS, TOK, HEAD), f32),
            pltpu.VMEM((2, SLOTS, TOK, HEAD), f32),
            pltpu.VMEM((2, 2, 4, TOK, HEAD), bf16),
            pltpu.VMEM((2, 2, 5, TOK, HEAD), bf16),
            dma((4, 2)),
            dma((5,)),
            dma((SLOTS,)),
            dma((2, 2, 5)),
            dma((2, 2, SLOTS)),
            dma((2, 2)),
            dma((2, 2)),
            dma((2, 2)),
            dma((2,)),
            dma((2, 2, 4)),
            dma((2, 2, 5)),
        ],
        compiler_params=pltpu.CompilerParams(
            collective_id=0, has_side_effects=True, vmem_limit_bytes=40 * 1024 * 1024
        ),
        cost_estimate=pl.CostEstimate(flops=2_700_000_000, bytes_accessed=4_000_000, transcendentals=2_097_152),
    )(query_rows, key_rows, value_matrix, out_grad, segments.reshape(1, TOK))


def solution(mesh):
    count, inner = mesh.size, mesh.shape["fsdp"]
    rows = P(("ctx", "fsdp"), None)
    return jax.shard_map(
        functools.partial(body, count, inner),
        mesh=mesh,
        in_specs=(rows, rows, rows, rows, P(("ctx", "fsdp"))),
        out_specs=(rows, rows, rows),
        check_vma=False,
    )
```

```python
import functools
import math

import jax
import jax.numpy as jnp
from jax import lax
from jax.experimental import pallas as pl
from jax.experimental.pallas import tpu as pltpu
from jax.sharding import PartitionSpec as P

HEAD = 128
GROUP = 8
TOK = 128
SLOTS = 5
WIDE = GROUP * HEAD
INV_ROOT = 1.0 / math.sqrt(HEAD)
TO_EXP2 = INV_ROOT * math.log2(math.e)
MESH = pl.DeviceIdType.MESH
NT = (((1,), (1,)), ((), ()))


def kernel(
    inner, count,
    q_in, k_in, v_in, o_in, seg_in,
    dq_out, dk_out, dv_out,
    qb, ob, kw, vw, segw, bias, pb, sb, dqs, acc_k, acc_v, stage, back,
    local_sem, seg_local, seg_send, seg_recv, kv_send, kv_recv, q_send, q_recv,
    dq_sem, dq_recv, back_send, back_recv,
):
    pos = lax.axis_index("ctx") * inner + lax.axis_index("fsdp")
    pairs = count // 2
    pair, core = pos // 2, pos % 2
    other = 1 - core

    def place(p):
        return (p // inner, p % inner)

    partner = 2 * pair + other
    has_next = pair + 1 < pairs
    has_next2 = jnp.logical_and(core == 1, pair + 2 < pairs)
    has_prev = pair >= 1
    has_prev2 = pair >= 2

    def kv_cols(h):
        return pl.ds(pl.multiple_of(h * HEAD, HEAD), HEAD)

    def q_cols(h):
        return pl.ds(pl.multiple_of(h * WIDE, WIDE), WIDE)

    own = []
    for gl in range(2):
        h = 2 * core + gl
        own.append(
            (
                pltpu.make_async_copy(k_in.at[:, kv_cols(h)], kw.at[gl, 3 + core], local_sem.at[0, gl]),
                pltpu.make_async_copy(v_in.at[:, kv_cols(h)], vw.at[gl, 3 + core], local_sem.at[1, gl]),
                pltpu.make_async_copy(q_in.at[:, q_cols(h)], qb.at[gl, core], local_sem.at[2, gl]),
                pltpu.make_async_copy(o_in.at[:, q_cols(h)], ob.at[gl, core], local_sem.at[3, gl]),
            )
        )

    barrier = pltpu.get_barrier_semaphore()

    def greet(p):
        pl.semaphore_signal(barrier, inc=1, device_id=place(p), device_id_type=MESH)

    greet(partner)

    @pl.when(has_next)
    def _():
        greet(2 * pair + 2)
        greet(2 * pair + 3)

    @pl.when(has_prev)
    def _():
        greet(2 * pair - 2)
        greet(2 * pair - 1)

    @pl.when(has_next2)
    def _():
        greet(2 * pair + 4)
        greet(2 * pair + 5)

    @pl.when(has_prev2)
    def _():
        greet(2 * pair - 3)

    for gl in range(2):
        for copy in own[gl]:
            copy.start()

    own_seg = pltpu.make_async_copy(seg_in, segw.at[3 + core], seg_local)
    own_seg.start()

    @pl.when(jnp.logical_not(has_prev2))
    def _():
        for gl in range(2):
            kw[gl, 0] = jnp.zeros((TOK, HEAD), jnp.bfloat16)
            vw[gl, 0] = jnp.zeros((TOK, HEAD), jnp.bfloat16)
        segw[0] = jnp.full((1, TOK), -1, jnp.int32)

    @pl.when(jnp.logical_not(has_prev))
    def _():
        for slot in (1, 2):
            for gl in range(2):
                kw[gl, slot] = jnp.zeros((TOK, HEAD), jnp.bfloat16)
                vw[gl, slot] = jnp.zeros((TOK, HEAD), jnp.bfloat16)
            segw[slot] = jnp.full((1, TOK), -1, jnp.int32)

    @pl.when(jnp.logical_not(has_next))
    def _():
        back[:, :, 0:2] = jnp.zeros((2, 2, 2, TOK, HEAD), jnp.bfloat16)

    @pl.when(jnp.logical_not(has_next2))
    def _():
        back[:, :, 2:4] = jnp.zeros((2, 2, 2, TOK, HEAD), jnp.bfloat16)

    signals = (
        1 + 2 * has_next.astype(jnp.int32) + 2 * has_prev.astype(jnp.int32)
        + 2 * has_next2.astype(jnp.int32) + has_prev2.astype(jnp.int32)
    )
    pl.semaphore_wait(barrier, signals)

    targets = [
        (0, 2 * pair + 2, has_next, 1 + core, 0),
        (1, 2 * pair + 3, has_next, 1 + core, 2),
        (2, 2 * pair + 4, has_next2, 0, 0),
        (3, 2 * pair + 5, has_next2, 0, 2),
        (4, partner, None, 3 + core, 2 * other),
    ]

    def guarded(cond, fn):
        if cond is None:
            fn()
        else:
            pl.when(cond)(fn)

    def seg_copy(target):
        n, p, _, slot, _ = target
        return pltpu.make_async_remote_copy(
            seg_in, segw.at[slot], seg_send.at[n], seg_recv.at[slot], place(p), MESH
        )

    def kv_copies(target, gl):
        n, p, _, slot, head = target
        cols = kv_cols(head + gl)
        return (
            pltpu.make_async_remote_copy(
                k_in.at[:, cols], kw.at[gl, slot], kv_send.at[0, gl, n], kv_recv.at[0, gl, slot], place(p), MESH
            ),
            pltpu.make_async_remote_copy(
                v_in.at[:, cols], vw.at[gl, slot], kv_send.at[1, gl, n], kv_recv.at[1, gl, slot], place(p), MESH
            ),
        )

    def q_copies(gl):
        cols = q_cols(2 * other + gl)
        return (
            pltpu.make_async_remote_copy(
                q_in.at[:, cols], qb.at[gl, core], q_send.at[0, gl], q_recv.at[0, gl], place(partner), MESH
            ),
            pltpu.make_async_remote_copy(
                o_in.at[:, cols], ob.at[gl, core], q_send.at[1, gl], q_recv.at[1, gl], place(partner), MESH
            ),
        )

    for target in targets:
        def start_seg(target=target):
            seg_copy(target).start()
        guarded(target[2], start_seg)
    def send_operands(gl):
        for target in targets:
            def start_kv(target=target, gl=gl):
                for copy in kv_copies(target, gl):
                    copy.start()
            guarded(target[2], start_kv)
        for copy in q_copies(gl):
            copy.start()

    send_operands(0)

    def landed(ref, sem):
        pltpu.make_async_remote_copy(ref, ref, sem, sem, place(partner), MESH).wait_recv()

    def near_arrivals(fn):
        def near():
            fn(1)
            fn(2)
        guarded(has_prev, near)
        fn(3 + other)

    def far_arrival(fn):
        guarded(has_prev2, lambda: fn(0))

    own_seg.wait()
    near_arrivals(lambda slot: landed(segw.at[slot], seg_recv.at[slot]))
    far_arrival(lambda slot: landed(segw.at[slot], seg_recv.at[slot]))
    row = lax.broadcasted_iota(jnp.int32, (TOK, TOK), 0)
    col = lax.broadcasted_iota(jnp.int32, (TOK, TOK), 1)
    key_seg = [
        jnp.broadcast_to(segw[slot, 0:1, :].astype(jnp.float32), (TOK, TOK)).T for slot in range(SLOTS)
    ]
    for t in range(2):
        query_seg = segw[3 + t, 0:1, :].astype(jnp.float32)
        for b in range(4):
            ok = key_seg[t + b] == query_seg
            if b == 0:
                ok = jnp.logical_and(ok, row > col)
            if b == 3:
                ok = jnp.logical_and(ok, row <= col)
            bias[t, b] = jnp.where(ok, 0.0, -1e30)

    def kv_landed(gl):
        def one(slot):
            landed(kw.at[gl, slot], kv_recv.at[0, gl, slot])
            landed(vw.at[gl, slot], kv_recv.at[1, gl, slot])
        return one

    def kv_wait_near(gl):
        own[gl][0].wait()
        own[gl][1].wait()
        near_arrivals(kv_landed(gl))

    def kv_wait_far(gl):
        far_arrival(kv_landed(gl))

    def q_wait(gl):
        own[gl][2].wait()
        own[gl][3].wait()
        landed(qb.at[gl, other], q_recv.at[0, gl])
        landed(ob.at[gl, other], q_recv.at[1, gl])

    def stacked(block):
        heads = block.shape[1] // HEAD
        return jnp.concatenate([block[:, i * HEAD : (i + 1) * HEAD] for i in range(heads)], 0)

    def dq_local(gl, t):
        cols = q_cols(2 * core + gl)
        return pltpu.make_async_copy(dqs.at[gl, t], dq_out.at[:, cols], dq_sem.at[gl, 0])

    def dq_remote(gl, t):
        cols = q_cols(2 * core + gl)
        return pltpu.make_async_remote_copy(
            dqs.at[gl, t], dq_out.at[:, cols], dq_sem.at[gl, 1], dq_recv.at[gl], place(partner), MESH
        )

    def probs_and_grads(gl, t):
        keys = kw[gl, t : t + 4].reshape(4 * TOK, HEAD)
        vals = vw[gl, t : t + 4].reshape(4 * TOK, HEAD)
        mask = bias[t].reshape(4 * TOK, TOK)
        mask = jnp.concatenate([mask, mask], 1)
        for hp in range(GROUP // 2):
            cols = slice(hp * 2 * HEAD, (hp + 1) * 2 * HEAD)
            q = stacked(qb[gl, t, :, cols])
            o = stacked(ob[gl, t, :, cols])
            s = lax.dot_general(keys, q, NT, preferred_element_type=jnp.float32) * TO_EXP2 + mask
            dp = lax.dot_general(vals, o, NT, preferred_element_type=jnp.float32)
            top = jnp.max(s, axis=0, keepdims=True)
            w = jnp.exp2(s - top)
            r = 1.0 / jnp.sum(w, axis=0, keepdims=True)
            delta = jnp.sum(w * dp, axis=0, keepdims=True) * r
            probs = w * r
            pb[:, cols] = probs.astype(jnp.bfloat16)
            sb[:, cols] = (probs * (dp - delta)).astype(jnp.bfloat16)

    def query_grads(gl, t):
        keys = kw[gl, t : t + 4].reshape(4 * TOK, HEAD)
        keys_t = keys.astype(jnp.float32).T.astype(jnp.bfloat16)
        for hp in range(GROUP // 2):
            cols = slice(hp * 2 * HEAD, (hp + 1) * 2 * HEAD)
            dq = (jnp.dot(keys_t, sb[:, cols], preferred_element_type=jnp.float32) * INV_ROOT).T
            dqs[gl, t, :, cols] = jnp.concatenate([dq[:TOK], dq[TOK:]], 1).astype(jnp.bfloat16)
        pl.when(core == t)(lambda: dq_local(gl, t).start())
        pl.when(core != t)(lambda: dq_remote(gl, t).start())

    def key_grads(gl, t, lower, upper, first):
        rows = slice(lower * TOK, upper * TOK)
        dk = jnp.dot(sb[rows], stacked(qb[gl, t]), preferred_element_type=jnp.float32) * INV_ROOT
        dv = jnp.dot(pb[rows], stacked(ob[gl, t]), preferred_element_type=jnp.float32)
        dk = dk.reshape(upper - lower, TOK, HEAD)
        dv = dv.reshape(upper - lower, TOK, HEAD)
        for b in range(lower, upper):
            slot = t + b
            if first or slot == 0 or slot == 4:
                acc_k[gl, slot] = dk[b - lower]
                acc_v[gl, slot] = dv[b - lower]
            else:
                acc_k[gl, slot] += dk[b - lower]
                acc_v[gl, slot] += dv[b - lower]

    homes = [
        (0, 2 * pair - 3, has_prev2, 0, 2 + core),
        (1, 2 * pair - 2, has_prev, 1, core),
        (2, 2 * pair - 1, has_prev, 2, core),
        (3, partner, None, 3 + other, 4),
    ]

    def back_copies(home, gl):
        n, p, _, slot, spot = home
        return [
            pltpu.make_async_remote_copy(
                stage.at[i, gl, n], back.at[i, gl, spot], back_send.at[i, gl, n],
                back_recv.at[i, gl, spot], place(p), MESH,
            )
            for i in range(2)
        ]

    def send_back(gl, numbers):
        for n in numbers:
            home = homes[n]
            slot = home[3]
            stage[0, gl, n] = acc_k[gl, slot].astype(jnp.bfloat16)
            stage[1, gl, n] = acc_v[gl, slot].astype(jnp.bfloat16)

            def start(home=home):
                for copy in back_copies(home, gl):
                    copy.start()
            guarded(home[2], start)

    kv_wait_near(0)
    q_wait(0)
    send_operands(1)
    probs_and_grads(0, 1)
    query_grads(0, 1)
    key_grads(0, 1, 0, 4, True)
    kv_wait_far(0)
    probs_and_grads(0, 0)
    key_grads(0, 0, 0, 4, False)
    send_back(0, (0, 1, 2, 3))
    query_grads(0, 0)
    kv_wait_near(1)
    kv_wait_far(1)
    q_wait(1)
    probs_and_grads(1, 0)
    key_grads(1, 0, 0, 4, True)
    send_back(1, (0,))
    query_grads(1, 0)
    probs_and_grads(1, 1)
    key_grads(1, 1, 0, 2, False)
    send_back(1, (1, 2))
    key_grads(1, 1, 2, 4, False)
    send_back(1, (3,))
    query_grads(1, 1)

    for gl in range(2):
        def near(gl=gl):
            for i in range(2):
                for spot in (0, 1):
                    landed(back.at[i, gl, spot], back_recv.at[i, gl, spot])
        guarded(has_next, near)

        def far(gl=gl):
            for i in range(2):
                for spot in (2, 3):
                    landed(back.at[i, gl, spot], back_recv.at[i, gl, spot])
        guarded(has_next2, far)
        for i in range(2):
            landed(back.at[i, gl, 4], back_recv.at[i, gl, 4])
        for i, acc, out in ((0, acc_k, dk_out), (1, acc_v, dv_out)):
            mine = acc[gl, 3 + core]
            mine += back[i, gl, core].astype(jnp.float32)
            mine += back[i, gl, 2 + core].astype(jnp.float32)
            out[:, kv_cols(2 * core + gl)] = mine.astype(jnp.bfloat16)
            rest = back[i, gl, 4].astype(jnp.float32)
            rest += back[i, gl, other].astype(jnp.float32)
            rest += back[i, gl, 2 + other].astype(jnp.float32)
            out[:, kv_cols(2 * other + gl)] = rest.astype(jnp.bfloat16)

    for target in targets:
        def sent(target=target):
            seg_copy(target).wait_send()
            for gl in range(2):
                for copy in kv_copies(target, gl):
                    copy.wait_send()
        guarded(target[2], sent)
    for gl in range(2):
        for copy in q_copies(gl):
            copy.wait_send()
        for home in homes:
            def returned(home=home, gl=gl):
                for copy in back_copies(home, gl):
                    copy.wait_send()
            guarded(home[2], returned)
        dq_local(gl, 0).wait()
        dq_remote(gl, 0).wait_send()
        landed(dq_out.at[:, q_cols(2 * other + gl)], dq_recv.at[gl])


def body(count, inner, query_rows, key_rows, value_matrix, out_grad, segments):
    bf16, f32 = jnp.bfloat16, jnp.float32
    dma = pltpu.SemaphoreType.DMA
    hbm = pl.BlockSpec(memory_space=pltpu.HBM)
    vmem = pl.BlockSpec(memory_space=pltpu.VMEM)
    return pl.pallas_call(
        functools.partial(kernel, inner, count),
        out_shape=(
            jax.ShapeDtypeStruct(query_rows.shape, bf16),
            jax.ShapeDtypeStruct(key_rows.shape, bf16),
            jax.ShapeDtypeStruct(value_matrix.shape, bf16),
        ),
        in_specs=[hbm] * 5,
        out_specs=(hbm, vmem, vmem),
        scratch_shapes=[
            pltpu.VMEM((2, 2, TOK, WIDE), bf16),
            pltpu.VMEM((2, 2, TOK, WIDE), bf16),
            pltpu.VMEM((2, SLOTS, TOK, HEAD), bf16),
            pltpu.VMEM((2, SLOTS, TOK, HEAD), bf16),
            pltpu.VMEM((SLOTS, 1, TOK), jnp.int32),
            pltpu.VMEM((2, 4, TOK, TOK), f32),
            pltpu.VMEM((4 * TOK, WIDE), bf16),
            pltpu.VMEM((4 * TOK, WIDE), bf16),
            pltpu.VMEM((2, 2, TOK, WIDE), bf16),
            pltpu.VMEM((2, SLOTS, TOK, HEAD), f32),
            pltpu.VMEM((2, SLOTS, TOK, HEAD), f32),
            pltpu.VMEM((2, 2, 4, TOK, HEAD), bf16),
            pltpu.VMEM((2, 2, 5, TOK, HEAD), bf16),
            dma((4, 2)),
            dma,
            dma((5,)),
            dma((SLOTS,)),
            dma((2, 2, 5)),
            dma((2, 2, SLOTS)),
            dma((2, 2)),
            dma((2, 2)),
            dma((2, 2)),
            dma((2,)),
            dma((2, 2, 4)),
            dma((2, 2, 5)),
        ],
        compiler_params=pltpu.CompilerParams(
            collective_id=0, has_side_effects=True, vmem_limit_bytes=63 * 1024 * 1024
        ),
        cost_estimate=pl.CostEstimate(flops=2_700_000_000, bytes_accessed=4_000_000, transcendentals=2_097_152),
    )(query_rows, key_rows, value_matrix, out_grad, segments.reshape(1, TOK))


def solution(mesh):
    count, inner = mesh.size, mesh.shape["fsdp"]
    rows = P(("ctx", "fsdp"), None)
    return jax.shard_map(
        functools.partial(body, count, inner),
        mesh=mesh,
        in_specs=(rows, rows, rows, rows, P(("ctx", "fsdp"))),
        out_specs=(rows, rows, rows),
        check_vma=False,
    )
```

```python
import functools
import math

import jax
import jax.numpy as jnp
from jax import lax
from jax.experimental import pallas as pl
from jax.experimental.pallas import tpu as pltpu
from jax.sharding import PartitionSpec as P

HEAD = 128
GROUP = 8
TOK = 128
SLOTS = 5
WIDE = GROUP * HEAD
INV_ROOT = 1.0 / math.sqrt(HEAD)
TO_EXP2 = INV_ROOT * math.log2(math.e)
MESH = pl.DeviceIdType.MESH
NT = (((1,), (1,)), ((), ()))


def kernel(
    inner, count,
    q_in, k_in, v_in, o_in, seg_in,
    dq_out, dk_out, dv_out,
    qb, ob, kw, vw, segw, bias, dqs, acc_k, acc_v, stage, back,
    local_sem, seg_local, seg_send, seg_recv, kv_send, kv_recv, q_send, q_recv,
    dq_sem, dq_recv, back_send, back_recv,
):
    pos = lax.axis_index("ctx") * inner + lax.axis_index("fsdp")
    pairs = count // 2
    pair, core = pos // 2, pos % 2
    other = 1 - core

    def place(p):
        return (p // inner, p % inner)

    partner = 2 * pair + other
    has_next = pair + 1 < pairs
    has_next2 = jnp.logical_and(core == 1, pair + 2 < pairs)
    has_prev = pair >= 1
    has_prev2 = pair >= 2

    def kv_cols(h):
        return pl.ds(pl.multiple_of(h * HEAD, HEAD), HEAD)

    def q_cols(h):
        return pl.ds(pl.multiple_of(h * WIDE, WIDE), WIDE)

    own = []
    for gl in range(2):
        h = 2 * core + gl
        own.append(
            (
                pltpu.make_async_copy(k_in.at[:, kv_cols(h)], kw.at[gl, 3 + core], local_sem.at[0, gl]),
                pltpu.make_async_copy(v_in.at[:, kv_cols(h)], vw.at[gl, 3 + core], local_sem.at[1, gl]),
                pltpu.make_async_copy(q_in.at[:, q_cols(h)], qb.at[gl, core], local_sem.at[2, gl]),
                pltpu.make_async_copy(o_in.at[:, q_cols(h)], ob.at[gl, core], local_sem.at[3, gl]),
            )
        )

    barrier = pltpu.get_barrier_semaphore()

    def greet(p):
        pl.semaphore_signal(barrier, inc=1, device_id=place(p), device_id_type=MESH)

    greet(partner)

    @pl.when(has_next)
    def _():
        greet(2 * pair + 2)
        greet(2 * pair + 3)

    @pl.when(has_prev)
    def _():
        greet(2 * pair - 2)
        greet(2 * pair - 1)

    @pl.when(has_next2)
    def _():
        greet(2 * pair + 4)
        greet(2 * pair + 5)

    @pl.when(has_prev2)
    def _():
        greet(2 * pair - 3)

    for gl in range(2):
        for copy in own[gl]:
            copy.start()

    own_seg = pltpu.make_async_copy(seg_in, segw.at[3 + core], seg_local)
    own_seg.start()

    @pl.when(jnp.logical_not(has_prev2))
    def _():
        for gl in range(2):
            kw[gl, 0] = jnp.zeros((TOK, HEAD), jnp.bfloat16)
            vw[gl, 0] = jnp.zeros((TOK, HEAD), jnp.bfloat16)
        segw[0] = jnp.full((1, TOK), -1, jnp.int32)

    @pl.when(jnp.logical_not(has_prev))
    def _():
        for slot in (1, 2):
            for gl in range(2):
                kw[gl, slot] = jnp.zeros((TOK, HEAD), jnp.bfloat16)
                vw[gl, slot] = jnp.zeros((TOK, HEAD), jnp.bfloat16)
            segw[slot] = jnp.full((1, TOK), -1, jnp.int32)

    @pl.when(jnp.logical_not(has_next))
    def _():
        back[:, :, 0:2] = jnp.zeros((2, 2, 2, TOK, HEAD), jnp.bfloat16)

    @pl.when(jnp.logical_not(has_next2))
    def _():
        back[:, :, 2:4] = jnp.zeros((2, 2, 2, TOK, HEAD), jnp.bfloat16)

    signals = (
        1 + 2 * has_next.astype(jnp.int32) + 2 * has_prev.astype(jnp.int32)
        + 2 * has_next2.astype(jnp.int32) + has_prev2.astype(jnp.int32)
    )
    pl.semaphore_wait(barrier, signals)

    targets = [
        (0, 2 * pair + 2, has_next, 1 + core, 0),
        (1, 2 * pair + 3, has_next, 1 + core, 2),
        (2, 2 * pair + 4, has_next2, 0, 0),
        (3, 2 * pair + 5, has_next2, 0, 2),
        (4, partner, None, 3 + core, 2 * other),
    ]

    def guarded(cond, fn):
        if cond is None:
            fn()
        else:
            pl.when(cond)(fn)

    def seg_copy(target):
        n, p, _, slot, _ = target
        return pltpu.make_async_remote_copy(
            seg_in, segw.at[slot], seg_send.at[n], seg_recv.at[slot], place(p), MESH
        )

    def kv_copies(target, gl):
        n, p, _, slot, head = target
        cols = kv_cols(head + gl)
        return (
            pltpu.make_async_remote_copy(
                k_in.at[:, cols], kw.at[gl, slot], kv_send.at[0, gl, n], kv_recv.at[0, gl, slot], place(p), MESH
            ),
            pltpu.make_async_remote_copy(
                v_in.at[:, cols], vw.at[gl, slot], kv_send.at[1, gl, n], kv_recv.at[1, gl, slot], place(p), MESH
            ),
        )

    def q_copies(gl):
        cols = q_cols(2 * other + gl)
        return (
            pltpu.make_async_remote_copy(
                q_in.at[:, cols], qb.at[gl, core], q_send.at[0, gl], q_recv.at[0, gl], place(partner), MESH
            ),
            pltpu.make_async_remote_copy(
                o_in.at[:, cols], ob.at[gl, core], q_send.at[1, gl], q_recv.at[1, gl], place(partner), MESH
            ),
        )

    for target in targets:
        def start_seg(target=target):
            seg_copy(target).start()
        guarded(target[2], start_seg)
    def send_operands(gl):
        for target in targets:
            def start_kv(target=target, gl=gl):
                for copy in kv_copies(target, gl):
                    copy.start()
            guarded(target[2], start_kv)
        for copy in q_copies(gl):
            copy.start()

    send_operands(0)

    def landed(ref, sem):
        pltpu.make_async_remote_copy(ref, ref, sem, sem, place(partner), MESH).wait_recv()

    def near_arrivals(fn):
        def near():
            fn(1)
            fn(2)
        guarded(has_prev, near)
        fn(3 + other)

    def far_arrival(fn):
        guarded(has_prev2, lambda: fn(0))

    own_seg.wait()
    near_arrivals(lambda slot: landed(segw.at[slot], seg_recv.at[slot]))
    far_arrival(lambda slot: landed(segw.at[slot], seg_recv.at[slot]))
    row = lax.broadcasted_iota(jnp.int32, (TOK, TOK), 0)
    col = lax.broadcasted_iota(jnp.int32, (TOK, TOK), 1)
    key_seg = [
        jnp.broadcast_to(segw[slot, 0:1, :].astype(jnp.float32), (TOK, TOK)).T for slot in range(SLOTS)
    ]
    for t in range(2):
        query_seg = segw[3 + t, 0:1, :].astype(jnp.float32)
        for b in range(4):
            ok = key_seg[t + b] == query_seg
            if b == 0:
                ok = jnp.logical_and(ok, row > col)
            if b == 3:
                ok = jnp.logical_and(ok, row <= col)
            bias[t, b] = jnp.where(ok, 0.0, -1e30)

    def kv_landed(gl):
        def one(slot):
            landed(kw.at[gl, slot], kv_recv.at[0, gl, slot])
            landed(vw.at[gl, slot], kv_recv.at[1, gl, slot])
        return one

    def kv_wait_near(gl):
        own[gl][0].wait()
        own[gl][1].wait()
        near_arrivals(kv_landed(gl))

    def kv_wait_far(gl):
        far_arrival(kv_landed(gl))

    def q_wait(gl):
        own[gl][2].wait()
        own[gl][3].wait()
        landed(qb.at[gl, other], q_recv.at[0, gl])
        landed(ob.at[gl, other], q_recv.at[1, gl])

    def stacked(block):
        heads = block.shape[1] // HEAD
        return jnp.concatenate([block[:, i * HEAD : (i + 1) * HEAD] for i in range(heads)], 0)

    def dq_local(gl, t):
        cols = q_cols(2 * core + gl)
        return pltpu.make_async_copy(dqs.at[gl, t], dq_out.at[:, cols], dq_sem.at[gl, 0])

    def dq_remote(gl, t):
        cols = q_cols(2 * core + gl)
        return pltpu.make_async_remote_copy(
            dqs.at[gl, t], dq_out.at[:, cols], dq_sem.at[gl, 1], dq_recv.at[gl], place(partner), MESH
        )

    def unit(gl, t, first, after):
        keys = kw[gl, t : t + 4].reshape(4 * TOK, HEAD)
        vals = vw[gl, t : t + 4].reshape(4 * TOK, HEAD)
        keys_t = keys.astype(jnp.float32).T.astype(jnp.bfloat16)
        mask = bias[t].reshape(4 * TOK, TOK)
        mask = jnp.concatenate([mask, mask], 1)
        pairs_of_heads = GROUP // 2

        def columns(hp):
            return slice(hp * 2 * HEAD, (hp + 1) * 2 * HEAD)

        def front(hp):
            q = stacked(qb[gl, t, :, columns(hp)])
            o = stacked(ob[gl, t, :, columns(hp)])
            s = lax.dot_general(keys, q, NT, preferred_element_type=jnp.float32) * TO_EXP2 + mask
            dp = lax.dot_general(vals, o, NT, preferred_element_type=jnp.float32)
            return s, dp

        def middle(s, dp):
            top = jnp.max(s, axis=0, keepdims=True)
            w = jnp.exp2(s - top)
            total = jnp.sum(w, axis=0, keepdims=True)
            delta = jnp.sum(w * dp, axis=0, keepdims=True) / total
            probs = jnp.exp2(s - (top + jnp.log2(total)))
            return probs.astype(jnp.bfloat16), (probs * (dp - delta)).astype(jnp.bfloat16)

        def rear(hp, probs, ds, sums):
            q = stacked(qb[gl, t, :, columns(hp)])
            o = stacked(ob[gl, t, :, columns(hp)])
            dk = jnp.dot(ds, q, preferred_element_type=jnp.float32)
            dv = jnp.dot(probs, o, preferred_element_type=jnp.float32)
            if sums is not None:
                dk, dv = sums[0] + dk, sums[1] + dv
            return dk, dv

        def query_side(hp, ds):
            dq = (jnp.dot(keys_t, ds, preferred_element_type=jnp.float32) * INV_ROOT).T
            dqs[gl, t, :, columns(hp)] = jnp.concatenate([dq[:TOK], dq[TOK:]], 1).astype(jnp.bfloat16)

        ready = front(0)
        sums, last = None, None
        for hp in range(pairs_of_heads):
            following = front(hp + 1) if hp + 1 < pairs_of_heads else None
            now = middle(*ready)
            if last is not None:
                sums = rear(hp - 1, *last, sums)
                query_side(hp - 1, last[1])
            ready, last = following, now
        dk, dv = rear(pairs_of_heads - 1, *last, sums)
        dk = (dk * INV_ROOT).reshape(4, TOK, HEAD)
        dv = dv.reshape(4, TOK, HEAD)
        for b in range(4):
            slot = t + b
            if first or slot == 0 or slot == 4:
                acc_k[gl, slot] = dk[b]
                acc_v[gl, slot] = dv[b]
            else:
                acc_k[gl, slot] += dk[b]
                acc_v[gl, slot] += dv[b]
        query_side(pairs_of_heads - 1, last[1])
        after()
        pl.when(core == t)(lambda: dq_local(gl, t).start())
        pl.when(core != t)(lambda: dq_remote(gl, t).start())

    homes = [
        (0, 2 * pair - 3, has_prev2, 0, 2 + core),
        (1, 2 * pair - 2, has_prev, 1, core),
        (2, 2 * pair - 1, has_prev, 2, core),
        (3, partner, None, 3 + other, 4),
    ]

    def back_copies(home, gl):
        n, p, _, slot, spot = home
        return [
            pltpu.make_async_remote_copy(
                stage.at[i, gl, n], back.at[i, gl, spot], back_send.at[i, gl, n],
                back_recv.at[i, gl, spot], place(p), MESH,
            )
            for i in range(2)
        ]

    def send_back(gl, numbers):
        for n in numbers:
            home = homes[n]
            slot = home[3]
            stage[0, gl, n] = acc_k[gl, slot].astype(jnp.bfloat16)
            stage[1, gl, n] = acc_v[gl, slot].astype(jnp.bfloat16)

            def start(home=home):
                for copy in back_copies(home, gl):
                    copy.start()
            guarded(home[2], start)

    kv_wait_near(0)
    q_wait(0)
    send_operands(1)
    unit(0, 1, True, lambda: None)
    kv_wait_far(0)
    unit(0, 0, False, lambda: send_back(0, (0, 1, 2, 3)))
    kv_wait_near(1)
    kv_wait_far(1)
    q_wait(1)
    unit(1, 0, True, lambda: send_back(1, (0,)))
    unit(1, 1, False, lambda: send_back(1, (1, 2, 3)))

    for gl in range(2):
        def near(gl=gl):
            for i in range(2):
                for spot in (0, 1):
                    landed(back.at[i, gl, spot], back_recv.at[i, gl, spot])
        guarded(has_next, near)

        def far(gl=gl):
            for i in range(2):
                for spot in (2, 3):
                    landed(back.at[i, gl, spot], back_recv.at[i, gl, spot])
        guarded(has_next2, far)
        for i in range(2):
            landed(back.at[i, gl, 4], back_recv.at[i, gl, 4])
        for i, acc, out in ((0, acc_k, dk_out), (1, acc_v, dv_out)):
            mine = acc[gl, 3 + core]
            mine += back[i, gl, core].astype(jnp.float32)
            mine += back[i, gl, 2 + core].astype(jnp.float32)
            out[:, kv_cols(2 * core + gl)] = mine.astype(jnp.bfloat16)
            rest = back[i, gl, 4].astype(jnp.float32)
            rest += back[i, gl, other].astype(jnp.float32)
            rest += back[i, gl, 2 + other].astype(jnp.float32)
            out[:, kv_cols(2 * other + gl)] = rest.astype(jnp.bfloat16)

    for target in targets:
        def sent(target=target):
            seg_copy(target).wait_send()
            for gl in range(2):
                for copy in kv_copies(target, gl):
                    copy.wait_send()
        guarded(target[2], sent)
    for gl in range(2):
        for copy in q_copies(gl):
            copy.wait_send()
        for home in homes:
            def returned(home=home, gl=gl):
                for copy in back_copies(home, gl):
                    copy.wait_send()
            guarded(home[2], returned)
        dq_local(gl, 0).wait()
        dq_remote(gl, 0).wait_send()
        landed(dq_out.at[:, q_cols(2 * other + gl)], dq_recv.at[gl])


def finish(dq, dk, dv, dq_out, dk_out, dv_out, sem):
    rows = TOK // 4
    copies = [
        pltpu.make_async_copy(dq.at[i * rows : (i + 1) * rows], dq_out.at[i * rows : (i + 1) * rows], sem.at[i])
        for i in range(4)
    ]
    copies.append(pltpu.make_async_copy(dk, dk_out, sem.at[4]))
    copies.append(pltpu.make_async_copy(dv, dv_out, sem.at[5]))
    for copy in copies:
        copy.start()
    for copy in copies:
        copy.wait()


def body(count, inner, query_rows, key_rows, value_matrix, out_grad, segments):
    bf16, f32 = jnp.bfloat16, jnp.float32
    dma = pltpu.SemaphoreType.DMA
    hbm = pl.BlockSpec(memory_space=pltpu.HBM)
    vmem = pl.BlockSpec(memory_space=pltpu.VMEM)
    parts = pl.pallas_call(
        functools.partial(kernel, inner, count),
        out_shape=(
            jax.ShapeDtypeStruct(query_rows.shape, bf16),
            jax.ShapeDtypeStruct(key_rows.shape, bf16),
            jax.ShapeDtypeStruct(value_matrix.shape, bf16),
        ),
        in_specs=[hbm] * 5,
        out_specs=(hbm, vmem, vmem),
        scratch_shapes=[
            pltpu.VMEM((2, 2, TOK, WIDE), bf16),
            pltpu.VMEM((2, 2, TOK, WIDE), bf16),
            pltpu.VMEM((2, SLOTS, TOK, HEAD), bf16),
            pltpu.VMEM((2, SLOTS, TOK, HEAD), bf16),
            pltpu.VMEM((SLOTS, 1, TOK), jnp.int32),
            pltpu.VMEM((2, 4, TOK, TOK), f32),
            pltpu.VMEM((2, 2, TOK, WIDE), bf16),
            pltpu.VMEM((2, SLOTS, TOK, HEAD), f32),
            pltpu.VMEM((2, SLOTS, TOK, HEAD), f32),
            pltpu.VMEM((2, 2, 4, TOK, HEAD), bf16),
            pltpu.VMEM((2, 2, 5, TOK, HEAD), bf16),
            dma((4, 2)),
            dma,
            dma((5,)),
            dma((SLOTS,)),
            dma((2, 2, 5)),
            dma((2, 2, SLOTS)),
            dma((2, 2)),
            dma((2, 2)),
            dma((2, 2)),
            dma((2,)),
            dma((2, 2, 4)),
            dma((2, 2, 5)),
        ],
        compiler_params=pltpu.CompilerParams(
            collective_id=0, has_side_effects=True, vmem_limit_bytes=63 * 1024 * 1024
        ),
        cost_estimate=pl.CostEstimate(flops=2_700_000_000, bytes_accessed=4_000_000, transcendentals=2_097_152),
    )(query_rows, key_rows, value_matrix, out_grad, segments.reshape(1, TOK))
    return pl.pallas_call(
        finish,
        out_shape=tuple(jax.ShapeDtypeStruct(part.shape, bf16) for part in parts),
        in_specs=[hbm] * 3,
        out_specs=(hbm,) * 3,
        scratch_shapes=[dma((6,))],
        compiler_params=pltpu.CompilerParams(vmem_limit_bytes=63 * 1024 * 1024),
    )(*parts)


def solution(mesh):
    count, inner = mesh.size, mesh.shape["fsdp"]
    rows = P(("ctx", "fsdp"), None)
    return jax.shard_map(
        functools.partial(body, count, inner),
        mesh=mesh,
        in_specs=(rows, rows, rows, rows, P(("ctx", "fsdp"))),
        out_specs=(rows, rows, rows),
        check_vma=False,
    )
```

```python
import functools
import math

import jax
import jax.numpy as jnp
from jax import lax
from jax.experimental import pallas as pl
from jax.experimental.pallas import tpu as pltpu
from jax.sharding import PartitionSpec as P

HEAD = 128
GROUP = 8
TOK = 128
SLOTS = 5
WIDE = GROUP * HEAD
INV_ROOT = 1.0 / math.sqrt(HEAD)
MESH = pl.DeviceIdType.MESH
NT = (((1,), (1,)), ((), ()))


def kernel(
    inner, count,
    q_in, k_in, v_in, o_in, seg_in,
    dq_out, dk_out, dv_out,
    qb, ob, kw, vw, segw, bias, dqs, acc_k, acc_v, stage, back,
    local_sem, seg_local, seg_send, seg_recv, kv_send, kv_recv, q_send, q_recv,
    dq_sem, dq_recv, back_send, back_recv,
):
    pos = lax.axis_index("ctx") * inner + lax.axis_index("fsdp")
    pairs = count // 2
    pair, core = pos // 2, pos % 2
    other = 1 - core

    def place(p):
        return (p // inner, p % inner)

    partner = 2 * pair + other
    has_next = pair + 1 < pairs
    has_next2 = jnp.logical_and(core == 1, pair + 2 < pairs)
    has_prev = pair >= 1
    has_prev2 = pair >= 2

    def kv_cols(h):
        return pl.ds(pl.multiple_of(h * HEAD, HEAD), HEAD)

    def q_cols(h):
        return pl.ds(pl.multiple_of(h * WIDE, WIDE), WIDE)

    own = []
    for gl in range(2):
        h = 2 * core + gl
        own.append(
            (
                pltpu.make_async_copy(k_in.at[:, kv_cols(h)], kw.at[gl, 3 + core], local_sem.at[0, gl]),
                pltpu.make_async_copy(v_in.at[:, kv_cols(h)], vw.at[gl, 3 + core], local_sem.at[1, gl]),
                pltpu.make_async_copy(q_in.at[:, q_cols(h)], qb.at[gl, core], local_sem.at[2, gl]),
                pltpu.make_async_copy(o_in.at[:, q_cols(h)], ob.at[gl, core], local_sem.at[3, gl]),
            )
        )

    barrier = pltpu.get_barrier_semaphore()

    def greet(p):
        pl.semaphore_signal(barrier, inc=1, device_id=place(p), device_id_type=MESH)

    greet(partner)

    @pl.when(has_next)
    def _():
        greet(2 * pair + 2)
        greet(2 * pair + 3)

    @pl.when(has_prev)
    def _():
        greet(2 * pair - 2)
        greet(2 * pair - 1)

    @pl.when(has_next2)
    def _():
        greet(2 * pair + 4)
        greet(2 * pair + 5)

    @pl.when(has_prev2)
    def _():
        greet(2 * pair - 3)

    for gl in range(2):
        for copy in own[gl]:
            copy.start()

    own_seg = pltpu.make_async_copy(seg_in, segw.at[3 + core], seg_local)
    own_seg.start()

    @pl.when(jnp.logical_not(has_prev2))
    def _():
        for gl in range(2):
            kw[gl, 0] = jnp.zeros((TOK, HEAD), jnp.bfloat16)
            vw[gl, 0] = jnp.zeros((TOK, HEAD), jnp.bfloat16)
        segw[0] = jnp.full((1, TOK), -1, jnp.int32)

    @pl.when(jnp.logical_not(has_prev))
    def _():
        for slot in (1, 2):
            for gl in range(2):
                kw[gl, slot] = jnp.zeros((TOK, HEAD), jnp.bfloat16)
                vw[gl, slot] = jnp.zeros((TOK, HEAD), jnp.bfloat16)
            segw[slot] = jnp.full((1, TOK), -1, jnp.int32)

    @pl.when(jnp.logical_not(has_next))
    def _():
        back[:, :, 0:2] = jnp.zeros((2, 2, 2, TOK, HEAD), jnp.bfloat16)

    @pl.when(jnp.logical_not(has_next2))
    def _():
        back[:, :, 2:4] = jnp.zeros((2, 2, 2, TOK, HEAD), jnp.bfloat16)

    signals = (
        1 + 2 * has_next.astype(jnp.int32) + 2 * has_prev.astype(jnp.int32)
        + 2 * has_next2.astype(jnp.int32) + has_prev2.astype(jnp.int32)
    )
    pl.semaphore_wait(barrier, signals)

    targets = [
        (0, 2 * pair + 2, has_next, 1 + core, 0),
        (1, 2 * pair + 3, has_next, 1 + core, 2),
        (2, 2 * pair + 4, has_next2, 0, 0),
        (3, 2 * pair + 5, has_next2, 0, 2),
        (4, partner, None, 3 + core, 2 * other),
    ]

    def guarded(cond, fn):
        if cond is None:
            fn()
        else:
            pl.when(cond)(fn)

    def seg_copy(target):
        n, p, _, slot, _ = target
        return pltpu.make_async_remote_copy(
            seg_in, segw.at[slot], seg_send.at[n], seg_recv.at[slot], place(p), MESH
        )

    def kv_copies(target, gl):
        n, p, _, slot, head = target
        cols = kv_cols(head + gl)
        return (
            pltpu.make_async_remote_copy(
                k_in.at[:, cols], kw.at[gl, slot], kv_send.at[0, gl, n], kv_recv.at[0, gl, slot], place(p), MESH
            ),
            pltpu.make_async_remote_copy(
                v_in.at[:, cols], vw.at[gl, slot], kv_send.at[1, gl, n], kv_recv.at[1, gl, slot], place(p), MESH
            ),
        )

    def q_copies(gl):
        cols = q_cols(2 * other + gl)
        return (
            pltpu.make_async_remote_copy(
                q_in.at[:, cols], qb.at[gl, core], q_send.at[0, gl], q_recv.at[0, gl], place(partner), MESH
            ),
            pltpu.make_async_remote_copy(
                o_in.at[:, cols], ob.at[gl, core], q_send.at[1, gl], q_recv.at[1, gl], place(partner), MESH
            ),
        )

    for target in targets:
        def start_seg(target=target):
            seg_copy(target).start()
        guarded(target[2], start_seg)
    def send_operands(gl, chosen):
        for target in chosen:
            def start_kv(target=target, gl=gl):
                for copy in kv_copies(target, gl):
                    copy.start()
            guarded(target[2], start_kv)

    def send_queries(gl):
        for copy in q_copies(gl):
            copy.start()

    send_operands(0, targets[:2] + targets[4:])
    send_queries(0)

    def landed(ref, sem):
        pltpu.make_async_remote_copy(ref, ref, sem, sem, place(partner), MESH).wait_recv()

    def near_arrivals(fn):
        def near():
            fn(1)
            fn(2)
        guarded(has_prev, near)
        fn(3 + other)

    def far_arrival(fn):
        guarded(has_prev2, lambda: fn(0))

    own_seg.wait()
    near_arrivals(lambda slot: landed(segw.at[slot], seg_recv.at[slot]))
    far_arrival(lambda slot: landed(segw.at[slot], seg_recv.at[slot]))
    row = lax.broadcasted_iota(jnp.int32, (TOK, TOK), 0)
    col = lax.broadcasted_iota(jnp.int32, (TOK, TOK), 1)
    key_seg = [
        jnp.broadcast_to(segw[slot, 0:1, :].astype(jnp.float32), (TOK, TOK)).T for slot in range(SLOTS)
    ]
    for t in range(2):
        query_seg = segw[3 + t, 0:1, :].astype(jnp.float32)
        for b in range(4):
            ok = key_seg[t + b] == query_seg
            if b == 0:
                ok = jnp.logical_and(ok, row > col)
            if b == 3:
                ok = jnp.logical_and(ok, row <= col)
            bias[t, b] = jnp.where(ok, 0.0, -1e30)

    def kv_landed(gl):
        def one(slot):
            landed(kw.at[gl, slot], kv_recv.at[0, gl, slot])
            landed(vw.at[gl, slot], kv_recv.at[1, gl, slot])
        return one

    def kv_wait_near(gl):
        own[gl][0].wait()
        own[gl][1].wait()
        near_arrivals(kv_landed(gl))

    def kv_wait_far(gl):
        far_arrival(kv_landed(gl))

    def q_wait(gl):
        own[gl][2].wait()
        own[gl][3].wait()
        landed(qb.at[gl, other], q_recv.at[0, gl])
        landed(ob.at[gl, other], q_recv.at[1, gl])

    def stacked(block):
        heads = block.shape[1] // HEAD
        return jnp.concatenate([block[:, i * HEAD : (i + 1) * HEAD] for i in range(heads)], 0)

    def dq_local(gl, t):
        cols = q_cols(2 * core + gl)
        return pltpu.make_async_copy(dqs.at[gl, t], dq_out.at[:, cols], dq_sem.at[gl, 0])

    def dq_remote(gl, t):
        cols = q_cols(2 * core + gl)
        return pltpu.make_async_remote_copy(
            dqs.at[gl, t], dq_out.at[:, cols], dq_sem.at[gl, 1], dq_recv.at[gl], place(partner), MESH
        )

    def unit(gl, t, first, after, split=False):
        keys = kw[gl, t : t + 4].reshape(4 * TOK, HEAD)
        vals = vw[gl, t : t + 4].reshape(4 * TOK, HEAD)
        keys_t = keys.astype(jnp.float32).T.astype(jnp.bfloat16)
        mask = bias[t].reshape(4 * TOK, TOK)
        mask = jnp.concatenate([mask, mask], 1)
        pairs_of_heads = GROUP // 2

        def columns(hp):
            return slice(hp * 2 * HEAD, (hp + 1) * 2 * HEAD)

        def front(hp):
            q = stacked(qb[gl, t, :, columns(hp)])
            o = stacked(ob[gl, t, :, columns(hp)])
            s = lax.dot_general(keys, q, NT, preferred_element_type=jnp.float32) * INV_ROOT + mask
            dp = lax.dot_general(vals, o, NT, preferred_element_type=jnp.float32)
            return s, dp

        def middle(s, dp):
            top = jnp.max(s, axis=0, keepdims=True)
            w = jnp.exp(s - top)
            total = jnp.sum(w, axis=0, keepdims=True)
            delta = jnp.sum(w * dp, axis=0, keepdims=True) / total
            probs = jnp.exp(s - (top + jnp.log(total)))
            return probs.astype(jnp.bfloat16), (probs * (dp - delta)).astype(jnp.bfloat16)

        def rear(hp, probs, ds, sums):
            q = stacked(qb[gl, t, :, columns(hp)])
            o = stacked(ob[gl, t, :, columns(hp)])
            dk = jnp.dot(ds, q, preferred_element_type=jnp.float32)
            dv = jnp.dot(probs, o, preferred_element_type=jnp.float32)
            if sums is not None:
                dk, dv = sums[0] + dk, sums[1] + dv
            return dk, dv

        def settle(dk, dv, lower):
            count = dk.shape[0] // TOK
            dk = (dk * INV_ROOT).reshape(count, TOK, HEAD)
            dv = dv.reshape(count, TOK, HEAD)
            for b in range(count):
                slot = t + lower + b
                if first or slot == 0 or slot == 4:
                    acc_k[gl, slot] = dk[b]
                    acc_v[gl, slot] = dv[b]
                else:
                    acc_k[gl, slot] += dk[b]
                    acc_v[gl, slot] += dv[b]

        def query_side(hp, ds):
            dq = (jnp.dot(keys_t, ds, preferred_element_type=jnp.float32) * INV_ROOT).T
            dqs[gl, t, :, columns(hp)] = jnp.concatenate([dq[:TOK], dq[TOK:]], 1).astype(jnp.bfloat16)

        ready = front(0)
        done = []
        sums = None
        for hp in range(pairs_of_heads):
            following = front(hp + 1) if hp + 1 < pairs_of_heads else None
            done.append(middle(*ready))
            if hp > 0 and not split:
                sums = rear(hp - 1, *done[hp - 1], sums)
                query_side(hp - 1, done[hp - 1][1])
            ready = following
        if split:
            probs = jnp.concatenate([d[0] for d in done], 1)
            ds = jnp.concatenate([d[1] for d in done], 1)
            q, o = stacked(qb[gl, t]), stacked(ob[gl, t])
            for lower in (0, 2):
                rows = slice(lower * TOK, (lower + 2) * TOK)
                dk = jnp.dot(ds[rows], q, preferred_element_type=jnp.float32)
                dv = jnp.dot(probs[rows], o, preferred_element_type=jnp.float32)
                settle(dk, dv, lower)
                after(lower)
            for hp in range(pairs_of_heads):
                query_side(hp, done[hp][1])
        else:
            sums = rear(pairs_of_heads - 1, *done[-1], sums)
            settle(*sums, 0)
            after(0)
            query_side(pairs_of_heads - 1, done[-1][1])
        pl.when(core == t)(lambda: dq_local(gl, t).start())
        pl.when(core != t)(lambda: dq_remote(gl, t).start())

    homes = [
        (0, 2 * pair - 3, has_prev2, 0, 2 + core),
        (1, 2 * pair - 2, has_prev, 1, core),
        (2, 2 * pair - 1, has_prev, 2, core),
        (3, partner, None, 3 + other, 4),
    ]

    def back_copies(home, gl):
        n, p, _, slot, spot = home
        return [
            pltpu.make_async_remote_copy(
                stage.at[i, gl, n], back.at[i, gl, spot], back_send.at[i, gl, n],
                back_recv.at[i, gl, spot], place(p), MESH,
            )
            for i in range(2)
        ]

    def send_back(gl, numbers):
        for n in numbers:
            home = homes[n]
            slot = home[3]
            stage[0, gl, n] = acc_k[gl, slot].astype(jnp.bfloat16)
            stage[1, gl, n] = acc_v[gl, slot].astype(jnp.bfloat16)

            def start(home=home):
                for copy in back_copies(home, gl):
                    copy.start()
            guarded(home[2], start)

    kv_wait_near(0)
    q_wait(0)
    send_operands(0, targets[2:4])
    send_operands(1, targets)
    send_queries(1)
    unit(0, 1, True, lambda lower: None)
    kv_wait_far(0)
    unit(0, 0, False, lambda lower: send_back(0, (0, 1, 2, 3)))
    kv_wait_near(1)
    kv_wait_far(1)
    q_wait(1)
    unit(1, 0, True, lambda lower: send_back(1, (0,)))
    unit(1, 1, False, lambda lower: send_back(1, (1, 2) if lower == 0 else (3,)), True)

    for gl in range(2):
        def near(gl=gl):
            for i in range(2):
                for spot in (0, 1):
                    landed(back.at[i, gl, spot], back_recv.at[i, gl, spot])
        guarded(has_next, near)

        def far(gl=gl):
            for i in range(2):
                for spot in (2, 3):
                    landed(back.at[i, gl, spot], back_recv.at[i, gl, spot])
        guarded(has_next2, far)
        for i in range(2):
            landed(back.at[i, gl, 4], back_recv.at[i, gl, 4])
        for i, acc, out in ((0, acc_k, dk_out), (1, acc_v, dv_out)):
            mine = acc[gl, 3 + core]
            mine += back[i, gl, core].astype(jnp.float32)
            mine += back[i, gl, 2 + core].astype(jnp.float32)
            out[:, kv_cols(2 * core + gl)] = mine.astype(jnp.bfloat16)
            rest = back[i, gl, 4].astype(jnp.float32)
            rest += back[i, gl, other].astype(jnp.float32)
            rest += back[i, gl, 2 + other].astype(jnp.float32)
            out[:, kv_cols(2 * other + gl)] = rest.astype(jnp.bfloat16)

    for target in targets:
        def sent(target=target):
            seg_copy(target).wait_send()
            for gl in range(2):
                for copy in kv_copies(target, gl):
                    copy.wait_send()
        guarded(target[2], sent)
    for gl in range(2):
        for copy in q_copies(gl):
            copy.wait_send()
        for home in homes:
            def returned(home=home, gl=gl):
                for copy in back_copies(home, gl):
                    copy.wait_send()
            guarded(home[2], returned)
        dq_local(gl, 0).wait()
        dq_remote(gl, 0).wait_send()
        landed(dq_out.at[:, q_cols(2 * other + gl)], dq_recv.at[gl])


def finish(dq, dk, dv, dq_out, dk_out, dv_out, dq_hold, kv_hold, in_sem, out_sem):
    rows = TOK // 4
    trips = []
    for i, (ref, out) in enumerate(((dk, dk_out), (dv, dv_out))):
        trips.append((ref, kv_hold.at[i], out))
    for i in range(4):
        part = pl.ds(i * rows, rows)
        trips.append((dq.at[part], dq_hold.at[part], dq_out.at[part]))
    inward = [pltpu.make_async_copy(ref, hold, in_sem.at[i]) for i, (ref, hold, _) in enumerate(trips)]
    outward = [pltpu.make_async_copy(hold, out, out_sem.at[i]) for i, (_, hold, out) in enumerate(trips)]
    for copy in inward:
        copy.start()
    for first, second in zip(inward, outward):
        first.wait()
        second.start()
    for copy in outward:
        copy.wait()


def body(count, inner, query_rows, key_rows, value_matrix, out_grad, segments):
    bf16, f32 = jnp.bfloat16, jnp.float32
    dma = pltpu.SemaphoreType.DMA
    hbm = pl.BlockSpec(memory_space=pltpu.HBM)
    vmem = pl.BlockSpec(memory_space=pltpu.VMEM)
    parts = pl.pallas_call(
        functools.partial(kernel, inner, count),
        out_shape=(
            jax.ShapeDtypeStruct(query_rows.shape, bf16),
            jax.ShapeDtypeStruct(key_rows.shape, bf16),
            jax.ShapeDtypeStruct(value_matrix.shape, bf16),
        ),
        in_specs=[hbm] * 5,
        out_specs=(hbm, vmem, vmem),
        scratch_shapes=[
            pltpu.VMEM((2, 2, TOK, WIDE), bf16),
            pltpu.VMEM((2, 2, TOK, WIDE), bf16),
            pltpu.VMEM((2, SLOTS, TOK, HEAD), bf16),
            pltpu.VMEM((2, SLOTS, TOK, HEAD), bf16),
            pltpu.VMEM((SLOTS, 1, TOK), jnp.int32),
            pltpu.VMEM((2, 4, TOK, TOK), f32),
            pltpu.VMEM((2, 2, TOK, WIDE), bf16),
            pltpu.VMEM((2, SLOTS, TOK, HEAD), f32),
            pltpu.VMEM((2, SLOTS, TOK, HEAD), f32),
            pltpu.VMEM((2, 2, 4, TOK, HEAD), bf16),
            pltpu.VMEM((2, 2, 5, TOK, HEAD), bf16),
            dma((4, 2)),
            dma,
            dma((5,)),
            dma((SLOTS,)),
            dma((2, 2, 5)),
            dma((2, 2, SLOTS)),
            dma((2, 2)),
            dma((2, 2)),
            dma((2, 2)),
            dma((2,)),
            dma((2, 2, 4)),
            dma((2, 2, 5)),
        ],
        compiler_params=pltpu.CompilerParams(
            collective_id=0, has_side_effects=True, vmem_limit_bytes=63 * 1024 * 1024
        ),
        cost_estimate=pl.CostEstimate(flops=2_700_000_000, bytes_accessed=4_000_000, transcendentals=2_097_152),
    )(query_rows, key_rows, value_matrix, out_grad, segments.reshape(1, TOK))
    return pl.pallas_call(
        finish,
        out_shape=tuple(jax.ShapeDtypeStruct(part.shape, bf16) for part in parts),
        in_specs=[hbm] * 3,
        out_specs=(hbm,) * 3,
        scratch_shapes=[
            pltpu.VMEM(query_rows.shape, bf16),
            pltpu.VMEM((2,) + key_rows.shape, bf16),
            dma((6,)),
            dma((6,)),
        ],
        compiler_params=pltpu.CompilerParams(vmem_limit_bytes=63 * 1024 * 1024),
    )(*parts)


def solution(mesh):
    count, inner = mesh.size, mesh.shape["fsdp"]
    rows = P(("ctx", "fsdp"), None)
    return jax.shard_map(
        functools.partial(body, count, inner),
        mesh=mesh,
        in_specs=(rows, rows, rows, rows, P(("ctx", "fsdp"))),
        out_specs=(rows, rows, rows),
        check_vma=False,
    )
```

```python
import functools
import math

import jax
import jax.numpy as jnp
from jax import lax
from jax.experimental import pallas as pl
from jax.experimental.pallas import tpu as pltpu
from jax.sharding import PartitionSpec as P

HEAD = 128
GROUP = 8
TOK = 128
SLOTS = 5
WIDE = GROUP * HEAD
INV_ROOT = 1.0 / math.sqrt(HEAD)
MESH = pl.DeviceIdType.MESH
NT = (((1,), (1,)), ((), ()))


def kernel(
    inner, count,
    q_in, k_in, v_in, o_in, seg_in,
    dq_out, dk_out, dv_out,
    qb, ob, kv, segw, bias, dqs, acc, stage, back,
    local_sem, seg_send, seg_recv, near_send, near_recv, far_send, far_recv, side_send, side_recv,
    q_send, q_recv, dq_sem, dq_recv, back_send, back_recv,
):
    pos = lax.axis_index("ctx") * inner + lax.axis_index("fsdp")
    pairs = count // 2
    pair, core = pos // 2, pos % 2
    other = 1 - core

    def place(p):
        return (p // inner, p % inner)

    partner = 2 * pair + other
    has_next = pair + 1 < pairs
    has_next2 = jnp.logical_and(core == 1, pair + 2 < pairs)
    has_prev = pair >= 1
    has_prev2 = pair >= 2

    def kv_cols(h):
        return pl.ds(pl.multiple_of(h * HEAD, HEAD), HEAD)

    def q_cols(h):
        return pl.ds(pl.multiple_of(h * WIDE, WIDE), WIDE)

    def both_cols(p):
        return pl.ds(pl.multiple_of(p * 2 * HEAD, 2 * HEAD), 2 * HEAD)

    def wide_cols(p):
        return pl.ds(pl.multiple_of(p * 2 * WIDE, 2 * WIDE), 2 * WIDE)

    own = (
        pltpu.make_async_copy(k_in.at[:, both_cols(core)], kv.at[3 + core, 0], local_sem.at[0]),
        pltpu.make_async_copy(v_in.at[:, both_cols(core)], kv.at[3 + core, 1], local_sem.at[1]),
        pltpu.make_async_copy(q_in.at[:, wide_cols(core)], qb.at[core], local_sem.at[2]),
        pltpu.make_async_copy(o_in.at[:, wide_cols(core)], ob.at[core], local_sem.at[3]),
        pltpu.make_async_copy(seg_in, segw.at[3 + core], local_sem.at[4]),
    )

    barrier = pltpu.get_barrier_semaphore()

    def greet(p):
        pl.semaphore_signal(barrier, inc=1, device_id=place(p), device_id_type=MESH)

    greet(partner)

    @pl.when(has_next)
    def _():
        greet(2 * pair + 2)
        greet(2 * pair + 3)

    @pl.when(has_prev)
    def _():
        greet(2 * pair - 2)
        greet(2 * pair - 1)

    @pl.when(has_next2)
    def _():
        greet(2 * pair + 4)
        greet(2 * pair + 5)

    @pl.when(has_prev2)
    def _():
        greet(2 * pair - 3)

    for copy in own:
        copy.start()

    @pl.when(jnp.logical_not(has_prev2))
    def _():
        kv[0] = jnp.zeros((2, TOK, 2 * HEAD), jnp.bfloat16)
        segw[0] = jnp.full((1, TOK), -1, jnp.int32)

    @pl.when(jnp.logical_not(has_prev))
    def _():
        kv[1:3] = jnp.zeros((2, 2, TOK, 2 * HEAD), jnp.bfloat16)
        segw[1:3] = jnp.full((2, 1, TOK), -1, jnp.int32)

    @pl.when(jnp.logical_not(has_next))
    def _():
        back[:, 0:2] = jnp.zeros((2, 2, 2, TOK, HEAD), jnp.bfloat16)

    @pl.when(jnp.logical_not(has_next2))
    def _():
        back[:, 2:4] = jnp.zeros((2, 2, 2, TOK, HEAD), jnp.bfloat16)

    signals = (
        1 + 2 * has_next.astype(jnp.int32) + 2 * has_prev.astype(jnp.int32)
        + 2 * has_next2.astype(jnp.int32) + has_prev2.astype(jnp.int32)
    )
    pl.semaphore_wait(barrier, signals)

    def remote(src, dst, send, recv, p):
        return pltpu.make_async_remote_copy(src, dst, send, recv, place(p), MESH)

    def guarded(cond, fn):
        if cond is None:
            fn()
        else:
            pl.when(cond)(fn)

    targets = [
        (0, 2 * pair + 2, has_next, 1 + core, 0),
        (1, 2 * pair + 3, has_next, 1 + core, 1),
        (2, 2 * pair + 4, has_next2, 0, 0),
        (3, 2 * pair + 5, has_next2, 0, 1),
        (4, partner, None, 3 + core, other),
    ]

    def seg_copy(target):
        n, p, _, slot, _ = target
        return remote(seg_in, segw.at[slot], seg_send.at[n], seg_recv.at[slot], p)

    def send_near(gl):
        def start():
            for _, p, _, slot, two in targets[:2]:
                for i, ref in ((0, k_in), (1, v_in)):
                    remote(
                        ref.at[:, kv_cols(2 * two + gl)], kv.at[slot, i, :, gl * HEAD : (gl + 1) * HEAD],
                        near_send, near_recv.at[gl], p,
                    ).start()
        guarded(has_next, start)

    def send_far():
        def start():
            for _, p, _, slot, two in targets[2:4]:
                for i, ref in ((0, k_in), (1, v_in)):
                    remote(ref.at[:, both_cols(two)], kv.at[slot, i], far_send, far_recv, p).start()
        guarded(has_next2, start)

    def send_side():
        for i, ref in ((0, k_in), (1, v_in)):
            remote(ref.at[:, both_cols(other)], kv.at[3 + core, i], side_send, side_recv, partner).start()
        remote(q_in.at[:, wide_cols(other)], qb.at[core], q_send.at[0], q_recv.at[0], partner).start()
        remote(o_in.at[:, wide_cols(other)], ob.at[core], q_send.at[1], q_recv.at[1], partner).start()

    for target in targets:
        def start_seg(target=target):
            seg_copy(target).start()
        guarded(target[2], start_seg)
    send_near(0)
    send_side()

    def landed(ref, sem):
        remote(ref, ref, sem, sem, partner).wait_recv()

    def left(ref, sem):
        remote(ref, ref, sem, sem, partner).wait_send()

    def wait_near(gl):
        guarded(has_prev, lambda: landed(kv.at[1:3, :, :, gl * HEAD : (gl + 1) * HEAD], near_recv.at[gl]))

    def wait_far():
        guarded(has_prev2, lambda: landed(kv.at[0], far_recv))

    def wait_side():
        for copy in own[:4]:
            copy.wait()
        landed(kv.at[3 + other], side_recv)
        landed(qb.at[other], q_recv.at[0])
        landed(ob.at[other], q_recv.at[1])

    own[4].wait()
    landed(segw.at[3 + other], seg_recv.at[3 + other])

    def seg_near():
        landed(segw.at[1], seg_recv.at[1])
        landed(segw.at[2], seg_recv.at[2])
    guarded(has_prev, seg_near)
    guarded(has_prev2, lambda: landed(segw.at[0], seg_recv.at[0]))
    row = lax.broadcasted_iota(jnp.int32, (TOK, TOK), 0)
    col = lax.broadcasted_iota(jnp.int32, (TOK, TOK), 1)
    key_seg = [
        jnp.broadcast_to(segw[slot, 0:1, :].astype(jnp.float32), (TOK, TOK)).T for slot in range(SLOTS)
    ]
    for t in range(2):
        query_seg = segw[3 + t, 0:1, :].astype(jnp.float32)
        merged = jnp.where(row > col, key_seg[t], key_seg[t + 3])
        for b, seg in enumerate((merged, key_seg[t + 1], key_seg[t + 2])):
            bias[t, b] = jnp.where(seg == query_seg, 0.0, -1e30)

    def stacked(block):
        heads = block.shape[1] // HEAD
        return jnp.concatenate([block[:, i * HEAD : (i + 1) * HEAD] for i in range(heads)], 0)

    def dq_local(gl, t):
        cols = q_cols(2 * core + gl)
        return pltpu.make_async_copy(dqs.at[gl, t], dq_out.at[:, cols], dq_sem.at[gl, 0])

    def dq_remote(gl, t):
        cols = q_cols(2 * core + gl)
        return pltpu.make_async_remote_copy(
            dqs.at[gl, t], dq_out.at[:, cols], dq_sem.at[gl, 1], dq_recv.at[gl], place(partner), MESH
        )

    def unit(gl, t, first, after):
        lanes = slice(gl * HEAD, (gl + 1) * HEAD)
        keys = kv[t : t + 4, 0, :, lanes].reshape(4 * TOK, HEAD)
        vals = kv[t : t + 4, 1, :, lanes].reshape(4 * TOK, HEAD)
        keys_t = keys.astype(jnp.float32).T.astype(jnp.bfloat16)
        mask = bias[t].reshape(3 * TOK, TOK)
        mask = jnp.concatenate([mask, mask], 1)
        upper = jnp.concatenate([row > col, row > col], 1)
        kept = upper.astype(jnp.float32).astype(jnp.bfloat16)
        rest = jnp.logical_not(upper).astype(jnp.float32).astype(jnp.bfloat16)
        pairs_of_heads = GROUP // 2

        def columns(hp):
            return slice((gl * GROUP + hp * 2) * HEAD, (gl * GROUP + hp * 2 + 2) * HEAD)

        def merge(x):
            return jnp.concatenate([jnp.where(upper, x[:TOK], x[3 * TOK :]), x[TOK : 3 * TOK]], 0)

        def spread(x):
            return jnp.concatenate([x[:TOK] * kept, x[TOK:], x[:TOK] * rest], 0)

        def front(hp):
            q = stacked(qb[t, :, columns(hp)])
            o = stacked(ob[t, :, columns(hp)])
            s = merge(lax.dot_general(keys, q, NT, preferred_element_type=jnp.float32)) * INV_ROOT + mask
            dp = merge(lax.dot_general(vals, o, NT, preferred_element_type=jnp.float32))
            return s, dp

        def middle(s, dp):
            top = jnp.max(s, axis=0, keepdims=True)
            w = jnp.exp(s - top)
            total = jnp.sum(w, axis=0, keepdims=True)
            delta = jnp.sum(w * dp, axis=0, keepdims=True) / total
            probs = jnp.exp(s - (top + jnp.log(total)))
            ds = (probs * (dp - delta)).astype(jnp.bfloat16)
            return spread(probs.astype(jnp.bfloat16)), spread(ds)

        def rear(hp, probs, ds, sums):
            q = stacked(qb[t, :, columns(hp)])
            o = stacked(ob[t, :, columns(hp)])
            dk = jnp.dot(ds, q, preferred_element_type=jnp.float32)
            dv = jnp.dot(probs, o, preferred_element_type=jnp.float32)
            if sums is not None:
                dk, dv = sums[0] + dk, sums[1] + dv
            return dk, dv

        def query_side(hp, ds):
            dq = (jnp.dot(keys_t, ds, preferred_element_type=jnp.float32) * INV_ROOT).T
            dqs[gl, t, :, hp * 2 * HEAD : (hp + 1) * 2 * HEAD] = jnp.concatenate([dq[:TOK], dq[TOK:]], 1).astype(jnp.bfloat16)

        ready = front(0)
        done = []
        sums = None
        for hp in range(pairs_of_heads):
            following = front(hp + 1) if hp + 1 < pairs_of_heads else None
            done.append(middle(*ready))
            if hp > 0:
                sums = rear(hp - 1, *done[hp - 1], sums)
                query_side(hp - 1, done[hp - 1][1])
            ready = following
        dk, dv = rear(pairs_of_heads - 1, *done[-1], sums)
        dk = (dk * INV_ROOT).reshape(4, TOK, HEAD)
        dv = dv.reshape(4, TOK, HEAD)
        for b in range(4):
            slot = t + b
            if first or slot == 0 or slot == 4:
                acc[gl, slot, 0] = dk[b]
                acc[gl, slot, 1] = dv[b]
            else:
                acc[gl, slot, 0] += dk[b]
                acc[gl, slot, 1] += dv[b]
        after()
        query_side(pairs_of_heads - 1, done[-1][1])
        pl.when(core == t)(lambda: dq_local(gl, t).start())
        pl.when(core != t)(lambda: dq_remote(gl, t).start())

    homes = [
        (0, 2 * pair - 3, has_prev2, 0, 2 + core),
        (1, 2 * pair - 2, has_prev, 1, core),
        (2, 2 * pair - 1, has_prev, 2, core),
        (3, partner, None, 3 + other, 4),
    ]

    def back_copy(home, gl):
        n, p, _, slot, spot = home
        return remote(stage.at[gl, n], back.at[gl, spot], back_send.at[gl, n], back_recv.at[gl, spot // 2], p)

    def send_back(gl, numbers):
        for n in numbers:
            home = homes[n]
            stage[gl, n] = acc[gl, home[3]].astype(jnp.bfloat16)
        for n in numbers:
            home = homes[n]

            def start(home=home):
                back_copy(home, gl).start()
            guarded(home[2], start)

    wait_side()
    wait_near(0)
    send_far()
    send_near(1)
    unit(0, 1, True, lambda: None)
    wait_far()
    unit(0, 0, False, lambda: send_back(0, (0, 1, 2, 3)))
    wait_near(1)
    unit(1, 0, True, lambda: send_back(1, (0,)))
    unit(1, 1, False, lambda: send_back(1, (1, 2, 3)))

    for target in targets:
        def sent(target=target):
            seg_copy(target).wait_send()
        guarded(target[2], sent)
    guarded(has_next, lambda: left(kv.at[0:2], near_send))
    guarded(has_next2, lambda: left(kv.at[0:2], far_send))
    left(kv.at[0], side_send)
    left(qb.at[0], q_send.at[0])
    left(ob.at[0], q_send.at[1])
    dq_local(0, 0).wait()
    dq_local(1, 0).wait()

    for gl in range(2):
        def near(gl=gl):
            landed(back.at[gl, 0:2], back_recv.at[gl, 0])
        guarded(has_next, near)

        def far(gl=gl):
            landed(back.at[gl, 2:4], back_recv.at[gl, 1])
        guarded(has_next2, far)
        landed(back.at[gl, 4], back_recv.at[gl, 2])
        for i, out in ((0, dk_out), (1, dv_out)):
            mine = acc[gl, 3 + core, i]
            mine += back[gl, core, i].astype(jnp.float32)
            mine += back[gl, 2 + core, i].astype(jnp.float32)
            out[:, kv_cols(2 * core + gl)] = mine.astype(jnp.bfloat16)
            theirs = back[gl, 4, i].astype(jnp.float32)
            theirs += back[gl, other, i].astype(jnp.float32)
            theirs += back[gl, 2 + other, i].astype(jnp.float32)
            out[:, kv_cols(2 * other + gl)] = theirs.astype(jnp.bfloat16)

    for gl in range(2):
        for home in homes:
            def returned(home=home, gl=gl):
                back_copy(home, gl).wait_send()
            guarded(home[2], returned)
        dq_remote(gl, 0).wait_send()
        landed(dq_out.at[:, q_cols(2 * other + gl)], dq_recv.at[gl])


def finish(dq, dk, dv, dq_out, dk_out, dv_out, dq_hold, kv_hold, in_sem, out_sem):
    rows = TOK // 4
    trips = []
    for i, (ref, out) in enumerate(((dk, dk_out), (dv, dv_out))):
        trips.append((ref, kv_hold.at[i], out))
    for i in range(4):
        part = pl.ds(i * rows, rows)
        trips.append((dq.at[part], dq_hold.at[part], dq_out.at[part]))
    inward = [pltpu.make_async_copy(ref, hold, in_sem.at[i]) for i, (ref, hold, _) in enumerate(trips)]
    outward = [pltpu.make_async_copy(hold, out, out_sem.at[i]) for i, (_, hold, out) in enumerate(trips)]
    for copy in inward:
        copy.start()
    for first, second in zip(inward, outward):
        first.wait()
        second.start()
    for copy in outward:
        copy.wait()


def body(count, inner, query_rows, key_rows, value_matrix, out_grad, segments):
    bf16, f32 = jnp.bfloat16, jnp.float32
    dma = pltpu.SemaphoreType.DMA
    hbm = pl.BlockSpec(memory_space=pltpu.HBM)
    vmem = pl.BlockSpec(memory_space=pltpu.VMEM)
    parts = pl.pallas_call(
        functools.partial(kernel, inner, count),
        out_shape=(
            jax.ShapeDtypeStruct(query_rows.shape, bf16),
            jax.ShapeDtypeStruct(key_rows.shape, bf16),
            jax.ShapeDtypeStruct(value_matrix.shape, bf16),
        ),
        in_specs=[hbm] * 5,
        out_specs=(hbm, vmem, vmem),
        scratch_shapes=[
            pltpu.VMEM((2, TOK, 2 * WIDE), bf16),
            pltpu.VMEM((2, TOK, 2 * WIDE), bf16),
            pltpu.VMEM((SLOTS, 2, TOK, 2 * HEAD), bf16),
            pltpu.VMEM((SLOTS, 1, TOK), jnp.int32),
            pltpu.VMEM((2, 3, TOK, TOK), f32),
            pltpu.VMEM((2, 2, TOK, WIDE), bf16),
            pltpu.VMEM((2, SLOTS, 2, TOK, HEAD), f32),
            pltpu.VMEM((2, 4, 2, TOK, HEAD), bf16),
            pltpu.VMEM((2, 5, 2, TOK, HEAD), bf16),
            dma((5,)),
            dma((5,)),
            dma((SLOTS,)),
            dma,
            dma((2,)),
            dma,
            dma,
            dma,
            dma,
            dma((2,)),
            dma((2,)),
            dma((2, 2)),
            dma((2,)),
            dma((2, 4)),
            dma((2, 3)),
        ],
        compiler_params=pltpu.CompilerParams(
            collective_id=0, has_side_effects=True, vmem_limit_bytes=63 * 1024 * 1024
        ),
        cost_estimate=pl.CostEstimate(flops=2_700_000_000, bytes_accessed=4_000_000, transcendentals=2_097_152),
    )(query_rows, key_rows, value_matrix, out_grad, segments.reshape(1, TOK))
    return pl.pallas_call(
        finish,
        out_shape=tuple(jax.ShapeDtypeStruct(part.shape, bf16) for part in parts),
        in_specs=[hbm] * 3,
        out_specs=(hbm,) * 3,
        scratch_shapes=[
            pltpu.VMEM(query_rows.shape, bf16),
            pltpu.VMEM((2,) + key_rows.shape, bf16),
            dma((6,)),
            dma((6,)),
        ],
        compiler_params=pltpu.CompilerParams(vmem_limit_bytes=63 * 1024 * 1024),
    )(*parts)


def solution(mesh):
    count, inner = mesh.size, mesh.shape["fsdp"]
    rows = P(("ctx", "fsdp"), None)
    return jax.shard_map(
        functools.partial(body, count, inner),
        mesh=mesh,
        in_specs=(rows, rows, rows, rows, P(("ctx", "fsdp"))),
        out_specs=(rows, rows, rows),
        check_vma=False,
    )
```

```python
import functools
import math

import jax
import jax.numpy as jnp
from jax import lax
from jax.experimental import pallas as pl
from jax.experimental.pallas import tpu as pltpu
from jax.sharding import PartitionSpec as P

HEAD = 128
GROUP = 8
TOK = 128
SLOTS = 5
WIDE = GROUP * HEAD
INV_ROOT = 1.0 / math.sqrt(HEAD)
MESH = pl.DeviceIdType.MESH
NT = (((1,), (1,)), ((), ()))


def kernel(
    inner, count,
    q_in, k_in, v_in, o_in, seg_in,
    dq_out, dk_out, dv_out,
    qb, ob, kv, segw, bias, dqs, acc, stage, back,
    local_sem, seg_send, seg_recv, near_send, near_recv, far_send, far_recv, side_send, side_recv,
    q_send, q_recv, dq_sem, dq_recv, back_send, back_recv,
):
    pos = lax.axis_index("ctx") * inner + lax.axis_index("fsdp")
    pairs = count // 2
    pair, core = pos // 2, pos % 2
    other = 1 - core

    def place(p):
        return (p // inner, p % inner)

    partner = 2 * pair + other
    has_next = pair + 1 < pairs
    has_next2 = jnp.logical_and(core == 1, pair + 2 < pairs)
    has_prev = pair >= 1
    has_prev2 = pair >= 2

    def kv_cols(h):
        return pl.ds(pl.multiple_of(h * HEAD, HEAD), HEAD)

    def q_cols(h):
        return pl.ds(pl.multiple_of(h * WIDE, WIDE), WIDE)

    def both_cols(p):
        return pl.ds(pl.multiple_of(p * 2 * HEAD, 2 * HEAD), 2 * HEAD)

    def wide_cols(p):
        return pl.ds(pl.multiple_of(p * 2 * WIDE, 2 * WIDE), 2 * WIDE)

    own = (
        pltpu.make_async_copy(k_in.at[:, both_cols(core)], kv.at[3 + core, 0], local_sem.at[0]),
        pltpu.make_async_copy(v_in.at[:, both_cols(core)], kv.at[3 + core, 1], local_sem.at[1]),
        pltpu.make_async_copy(q_in.at[:, wide_cols(core)], qb.at[core], local_sem.at[2]),
        pltpu.make_async_copy(o_in.at[:, wide_cols(core)], ob.at[core], local_sem.at[3]),
        pltpu.make_async_copy(seg_in, segw.at[3 + core], local_sem.at[4]),
    )

    barrier = pltpu.get_barrier_semaphore()

    def greet(p):
        pl.semaphore_signal(barrier, inc=1, device_id=place(p), device_id_type=MESH)

    greet(partner)

    @pl.when(has_next)
    def _():
        greet(2 * pair + 2)
        greet(2 * pair + 3)

    @pl.when(has_prev)
    def _():
        greet(2 * pair - 2)
        greet(2 * pair - 1)

    @pl.when(has_next2)
    def _():
        greet(2 * pair + 4)
        greet(2 * pair + 5)

    @pl.when(has_prev2)
    def _():
        greet(2 * pair - 3)

    for copy in own:
        copy.start()

    @pl.when(jnp.logical_not(has_prev2))
    def _():
        kv[0] = jnp.zeros((2, TOK, 2 * HEAD), jnp.bfloat16)
        segw[0] = jnp.full((1, TOK), -1, jnp.int32)

    @pl.when(jnp.logical_not(has_prev))
    def _():
        kv[1:3] = jnp.zeros((2, 2, TOK, 2 * HEAD), jnp.bfloat16)
        segw[1:3] = jnp.full((2, 1, TOK), -1, jnp.int32)

    @pl.when(jnp.logical_not(has_next))
    def _():
        back[:, 0:2] = jnp.zeros((2, 2, 2, TOK, HEAD), jnp.bfloat16)

    @pl.when(jnp.logical_not(has_next2))
    def _():
        back[:, 2:4] = jnp.zeros((2, 2, 2, TOK, HEAD), jnp.bfloat16)

    signals = (
        1 + 2 * has_next.astype(jnp.int32) + 2 * has_prev.astype(jnp.int32)
        + 2 * has_next2.astype(jnp.int32) + has_prev2.astype(jnp.int32)
    )
    pl.semaphore_wait(barrier, signals)

    def remote(src, dst, send, recv, p):
        return pltpu.make_async_remote_copy(src, dst, send, recv, place(p), MESH)

    def guarded(cond, fn):
        if cond is None:
            fn()
        else:
            pl.when(cond)(fn)

    targets = [
        (0, 2 * pair + 2, has_next, 1 + core, 0),
        (1, 2 * pair + 3, has_next, 1 + core, 1),
        (2, 2 * pair + 4, has_next2, 0, 0),
        (3, 2 * pair + 5, has_next2, 0, 1),
        (4, partner, None, 3 + core, other),
    ]

    def seg_copy(target):
        n, p, _, slot, _ = target
        return remote(seg_in, segw.at[slot], seg_send.at[n], seg_recv.at[slot], p)

    def send_near(gl):
        def start():
            for _, p, _, slot, two in targets[:2]:
                for i, ref in ((0, k_in), (1, v_in)):
                    remote(
                        ref.at[:, kv_cols(2 * two + gl)], kv.at[slot, i, :, gl * HEAD : (gl + 1) * HEAD],
                        near_send, near_recv.at[gl], p,
                    ).start()
        guarded(has_next, start)

    def send_far():
        def start():
            for _, p, _, slot, two in targets[2:4]:
                for i, ref in ((0, k_in), (1, v_in)):
                    remote(ref.at[:, both_cols(two)], kv.at[slot, i], far_send, far_recv, p).start()
        guarded(has_next2, start)

    def send_side():
        for i, ref in ((0, k_in), (1, v_in)):
            remote(ref.at[:, both_cols(other)], kv.at[3 + core, i], side_send, side_recv, partner).start()
        remote(q_in.at[:, wide_cols(other)], qb.at[core], q_send.at[0], q_recv.at[0], partner).start()
        remote(o_in.at[:, wide_cols(other)], ob.at[core], q_send.at[1], q_recv.at[1], partner).start()

    for target in targets:
        def start_seg(target=target):
            seg_copy(target).start()
        guarded(target[2], start_seg)
    send_near(0)
    send_side()

    def landed(ref, sem):
        remote(ref, ref, sem, sem, partner).wait_recv()

    def left(ref, sem):
        remote(ref, ref, sem, sem, partner).wait_send()

    def wait_near(gl):
        guarded(has_prev, lambda: landed(kv.at[1:3, :, :, gl * HEAD : (gl + 1) * HEAD], near_recv.at[gl]))

    def wait_far():
        guarded(has_prev2, lambda: landed(kv.at[0], far_recv))

    def wait_side():
        for copy in own[:4]:
            copy.wait()
        landed(kv.at[3 + other], side_recv)
        landed(qb.at[other], q_recv.at[0])
        landed(ob.at[other], q_recv.at[1])

    own[4].wait()
    landed(segw.at[3 + other], seg_recv.at[3 + other])

    def seg_near():
        landed(segw.at[1], seg_recv.at[1])
        landed(segw.at[2], seg_recv.at[2])
    guarded(has_prev, seg_near)
    guarded(has_prev2, lambda: landed(segw.at[0], seg_recv.at[0]))
    row = lax.broadcasted_iota(jnp.int32, (TOK, TOK), 0)
    col = lax.broadcasted_iota(jnp.int32, (TOK, TOK), 1)
    key_seg = [
        jnp.broadcast_to(segw[slot, 0:1, :].astype(jnp.float32), (TOK, TOK)).T for slot in range(SLOTS)
    ]
    for t in range(2):
        query_seg = segw[3 + t, 0:1, :].astype(jnp.float32)
        merged = jnp.where(row > col, key_seg[t], key_seg[t + 3])
        for b, seg in enumerate((merged, key_seg[t + 1], key_seg[t + 2])):
            bias[t, b] = jnp.where(seg == query_seg, 0.0, -1e30)

    def stacked(block):
        heads = block.shape[1] // HEAD
        return jnp.concatenate([block[:, i * HEAD : (i + 1) * HEAD] for i in range(heads)], 0)

    def dq_local(gl, t):
        cols = q_cols(2 * core + gl)
        return pltpu.make_async_copy(dqs.at[gl, t], dq_out.at[:, cols], dq_sem.at[gl, 0])

    def dq_remote(gl, t):
        cols = q_cols(2 * core + gl)
        return pltpu.make_async_remote_copy(
            dqs.at[gl, t], dq_out.at[:, cols], dq_sem.at[gl, 1], dq_recv.at[gl], place(partner), MESH
        )

    def unit(gl, t, first, after, last=None):
        lanes = slice(gl * HEAD, (gl + 1) * HEAD)
        keys = kv[t : t + 4, 0, :, lanes].reshape(4 * TOK, HEAD)
        vals = kv[t : t + 4, 1, :, lanes].reshape(4 * TOK, HEAD)
        keys_t = keys.astype(jnp.float32).T.astype(jnp.bfloat16)
        mask = bias[t].reshape(3 * TOK, TOK)
        mask = jnp.concatenate([mask, mask], 1)
        upper = jnp.concatenate([row > col, row > col], 1)
        kept = upper.astype(jnp.float32).astype(jnp.bfloat16)
        rest = jnp.logical_not(upper).astype(jnp.float32).astype(jnp.bfloat16)
        pairs_of_heads = GROUP // 2

        def columns(hp):
            return slice((gl * GROUP + hp * 2) * HEAD, (gl * GROUP + hp * 2 + 2) * HEAD)

        def merge(x):
            return jnp.concatenate([jnp.where(upper, x[:TOK], x[3 * TOK :]), x[TOK : 3 * TOK]], 0)

        def spread(x):
            return jnp.concatenate([x[:TOK] * kept, x[TOK:], x[:TOK] * rest], 0)

        def front(hp):
            q = stacked(qb[t, :, columns(hp)])
            o = stacked(ob[t, :, columns(hp)])
            s = merge(lax.dot_general(keys, q, NT, preferred_element_type=jnp.float32)) * INV_ROOT + mask
            dp = merge(lax.dot_general(vals, o, NT, preferred_element_type=jnp.float32))
            return s, dp

        def middle(s, dp):
            top = jnp.max(s, axis=0, keepdims=True)
            w = jnp.exp(s - top)
            scale = 1.0 / jnp.sum(w, axis=0, keepdims=True)
            delta = jnp.sum(w * dp, axis=0, keepdims=True) * scale
            probs = w * scale
            ds = (probs * (dp - delta)).astype(jnp.bfloat16)
            return spread(probs.astype(jnp.bfloat16)), spread(ds)

        def rear(hp, probs, ds, sums, rows):
            q = stacked(qb[t, :, columns(hp)])
            o = stacked(ob[t, :, columns(hp)])
            dk = jnp.dot(ds[rows], q, preferred_element_type=jnp.float32)
            dv = jnp.dot(probs[rows], o, preferred_element_type=jnp.float32)
            if sums is not None:
                dk, dv = sums[0] + dk, sums[1] + dv
            return dk, dv

        def settle(sums, lower):
            count = sums[0].shape[0] // TOK
            dk = (sums[0] * INV_ROOT).reshape(count, TOK, HEAD)
            dv = sums[1].reshape(count, TOK, HEAD)
            for b in range(count):
                slot = t + lower + b
                if first or slot == 0 or slot == 4:
                    acc[gl, slot, 0] = dk[b]
                    acc[gl, slot, 1] = dv[b]
                else:
                    acc[gl, slot, 0] += dk[b]
                    acc[gl, slot, 1] += dv[b]

        def query_side(hp, ds):
            dq = (jnp.dot(keys_t, ds, preferred_element_type=jnp.float32) * INV_ROOT).T
            dqs[gl, t, :, hp * 2 * HEAD : (hp + 1) * 2 * HEAD] = jnp.concatenate([dq[:TOK], dq[TOK:]], 1).astype(jnp.bfloat16)

        ready = front(0)
        done = []
        sums = None
        split = last is not None
        early = slice(0, 2 * TOK) if split else slice(0, 4 * TOK)
        late = slice(2 * TOK, 4 * TOK)
        for hp in range(pairs_of_heads):
            following = front(hp + 1) if hp + 1 < pairs_of_heads else None
            done.append(middle(*ready))
            if hp > 0:
                sums = rear(hp - 1, *done[hp - 1], sums, early)
                if not split:
                    query_side(hp - 1, done[hp - 1][1])
            ready = following
        sums = rear(pairs_of_heads - 1, *done[-1], sums, early)
        settle(sums, 0)
        after()
        if split:
            sums = None
            for hp in range(pairs_of_heads):
                sums = rear(hp, *done[hp], sums, late)
                query_side(hp, done[hp][1])
            settle(sums, 2)
            last()
        else:
            query_side(pairs_of_heads - 1, done[-1][1])
        pl.when(core == t)(lambda: dq_local(gl, t).start())
        pl.when(core != t)(lambda: dq_remote(gl, t).start())

    homes = [
        (0, 2 * pair - 3, has_prev2, 0, 2 + core),
        (1, 2 * pair - 2, has_prev, 1, core),
        (2, 2 * pair - 1, has_prev, 2, core),
        (3, partner, None, 3 + other, 4),
    ]

    def back_copy(home, gl):
        n, p, _, slot, spot = home
        return remote(stage.at[gl, n], back.at[gl, spot], back_send.at[gl, n], back_recv.at[gl, spot // 2], p)

    def send_back(gl, numbers):
        for n in numbers:
            home = homes[n]
            stage[gl, n] = acc[gl, home[3]].astype(jnp.bfloat16)
        for n in numbers:
            home = homes[n]

            def start(home=home):
                back_copy(home, gl).start()
            guarded(home[2], start)

    wait_side()
    wait_near(0)
    send_far()
    send_near(1)
    unit(0, 1, True, lambda: None)
    wait_far()
    unit(0, 0, False, lambda: send_back(0, (0, 1, 2, 3)))
    wait_near(1)
    unit(1, 0, True, lambda: send_back(1, (0,)))
    unit(1, 1, False, lambda: send_back(1, (1, 2)), lambda: send_back(1, (3,)))

    for target in targets:
        def sent(target=target):
            seg_copy(target).wait_send()
        guarded(target[2], sent)
    guarded(has_next, lambda: left(kv.at[0:2], near_send))
    guarded(has_next2, lambda: left(kv.at[0:2], far_send))
    left(kv.at[0], side_send)
    left(qb.at[0], q_send.at[0])
    left(ob.at[0], q_send.at[1])
    dq_local(0, 0).wait()
    dq_local(1, 0).wait()

    for gl in range(2):
        def near(gl=gl):
            landed(back.at[gl, 0:2], back_recv.at[gl, 0])
        guarded(has_next, near)

        def far(gl=gl):
            landed(back.at[gl, 2:4], back_recv.at[gl, 1])
        guarded(has_next2, far)
        landed(back.at[gl, 4], back_recv.at[gl, 2])
        for i, out in ((0, dk_out), (1, dv_out)):
            mine = acc[gl, 3 + core, i]
            mine += back[gl, core, i].astype(jnp.float32)
            mine += back[gl, 2 + core, i].astype(jnp.float32)
            out[:, kv_cols(2 * core + gl)] = mine.astype(jnp.bfloat16)
            theirs = back[gl, 4, i].astype(jnp.float32)
            theirs += back[gl, other, i].astype(jnp.float32)
            theirs += back[gl, 2 + other, i].astype(jnp.float32)
            out[:, kv_cols(2 * other + gl)] = theirs.astype(jnp.bfloat16)

    for gl in range(2):
        for home in homes:
            def returned(home=home, gl=gl):
                back_copy(home, gl).wait_send()
            guarded(home[2], returned)
        dq_remote(gl, 0).wait_send()
        landed(dq_out.at[:, q_cols(2 * other + gl)], dq_recv.at[gl])


def finish(dq, dk, dv, dq_out, dk_out, dv_out, dq_hold, kv_hold, in_sem, out_sem):
    rows = TOK // 4
    trips = []
    for i, (ref, out) in enumerate(((dk, dk_out), (dv, dv_out))):
        trips.append((ref, kv_hold.at[i], out))
    for i in range(4):
        part = pl.ds(i * rows, rows)
        trips.append((dq.at[part], dq_hold.at[part], dq_out.at[part]))
    inward = [pltpu.make_async_copy(ref, hold, in_sem.at[i]) for i, (ref, hold, _) in enumerate(trips)]
    outward = [pltpu.make_async_copy(hold, out, out_sem.at[i]) for i, (_, hold, out) in enumerate(trips)]
    for copy in inward:
        copy.start()
    for first, second in zip(inward, outward):
        first.wait()
        second.start()
    for copy in outward:
        copy.wait()


def body(count, inner, query_rows, key_rows, value_matrix, out_grad, segments):
    bf16, f32 = jnp.bfloat16, jnp.float32
    dma = pltpu.SemaphoreType.DMA
    hbm = pl.BlockSpec(memory_space=pltpu.HBM)
    vmem = pl.BlockSpec(memory_space=pltpu.VMEM)
    parts = pl.pallas_call(
        functools.partial(kernel, inner, count),
        out_shape=(
            jax.ShapeDtypeStruct(query_rows.shape, bf16),
            jax.ShapeDtypeStruct(key_rows.shape, bf16),
            jax.ShapeDtypeStruct(value_matrix.shape, bf16),
        ),
        in_specs=[hbm] * 5,
        out_specs=(hbm, vmem, vmem),
        scratch_shapes=[
            pltpu.VMEM((2, TOK, 2 * WIDE), bf16),
            pltpu.VMEM((2, TOK, 2 * WIDE), bf16),
            pltpu.VMEM((SLOTS, 2, TOK, 2 * HEAD), bf16),
            pltpu.VMEM((SLOTS, 1, TOK), jnp.int32),
            pltpu.VMEM((2, 3, TOK, TOK), f32),
            pltpu.VMEM((2, 2, TOK, WIDE), bf16),
            pltpu.VMEM((2, SLOTS, 2, TOK, HEAD), f32),
            pltpu.VMEM((2, 4, 2, TOK, HEAD), bf16),
            pltpu.VMEM((2, 5, 2, TOK, HEAD), bf16),
            dma((5,)),
            dma((5,)),
            dma((SLOTS,)),
            dma,
            dma((2,)),
            dma,
            dma,
            dma,
            dma,
            dma((2,)),
            dma((2,)),
            dma((2, 2)),
            dma((2,)),
            dma((2, 4)),
            dma((2, 3)),
        ],
        compiler_params=pltpu.CompilerParams(
            collective_id=0, has_side_effects=True, vmem_limit_bytes=63 * 1024 * 1024
        ),
        cost_estimate=pl.CostEstimate(flops=2_700_000_000, bytes_accessed=4_000_000, transcendentals=2_097_152),
    )(query_rows, key_rows, value_matrix, out_grad, segments.reshape(1, TOK))
    return pl.pallas_call(
        finish,
        out_shape=tuple(jax.ShapeDtypeStruct(part.shape, bf16) for part in parts),
        in_specs=[hbm] * 3,
        out_specs=(hbm,) * 3,
        scratch_shapes=[
            pltpu.VMEM(query_rows.shape, bf16),
            pltpu.VMEM((2,) + key_rows.shape, bf16),
            dma((6,)),
            dma((6,)),
        ],
        compiler_params=pltpu.CompilerParams(vmem_limit_bytes=63 * 1024 * 1024),
    )(*parts)


def solution(mesh):
    count, inner = mesh.size, mesh.shape["fsdp"]
    rows = P(("ctx", "fsdp"), None)
    return jax.shard_map(
        functools.partial(body, count, inner),
        mesh=mesh,
        in_specs=(rows, rows, rows, rows, P(("ctx", "fsdp"))),
        out_specs=(rows, rows, rows),
        check_vma=False,
    )
```

```python
import functools
import math

import jax
import jax.numpy as jnp
from jax import lax
from jax.experimental import pallas as pl
from jax.experimental.pallas import tpu as pltpu
from jax.sharding import PartitionSpec as P

HEAD = 128
GROUP = 8
TOK = 128
SLOTS = 5
WIDE = GROUP * HEAD
INV_ROOT = 1.0 / math.sqrt(HEAD)
MESH = pl.DeviceIdType.MESH
NT = (((1,), (1,)), ((), ()))


def kernel(
    inner, count,
    q_in, k_in, v_in, o_in, seg_in,
    dq_out, dk_out, dv_out,
    qb, ob, kv, segw, bias, dqs, acc, stage, back,
    local_sem, seg_send, seg_recv, near_send, near_recv, far_send, far_recv, side_send, side_recv,
    q_send, q_recv, dq_sem, dq_recv, back_send, back_recv,
):
    pos = lax.axis_index("ctx") * inner + lax.axis_index("fsdp")
    pairs = count // 2
    pair, core = pos // 2, pos % 2
    other = 1 - core

    def place(p):
        return (p // inner, p % inner)

    partner = 2 * pair + other
    has_next = pair + 1 < pairs
    has_next2 = jnp.logical_and(core == 1, pair + 2 < pairs)
    has_prev = pair >= 1
    has_prev2 = pair >= 2

    def kv_cols(h):
        return pl.ds(pl.multiple_of(h * HEAD, HEAD), HEAD)

    def q_cols(h):
        return pl.ds(pl.multiple_of(h * WIDE, WIDE), WIDE)

    def both_cols(p):
        return pl.ds(pl.multiple_of(p * 2 * HEAD, 2 * HEAD), 2 * HEAD)

    def wide_cols(p):
        return pl.ds(pl.multiple_of(p * 2 * WIDE, 2 * WIDE), 2 * WIDE)

    own = (
        pltpu.make_async_copy(k_in.at[:, both_cols(core)], kv.at[3 + core, 0], local_sem.at[0]),
        pltpu.make_async_copy(v_in.at[:, both_cols(core)], kv.at[3 + core, 1], local_sem.at[1]),
        pltpu.make_async_copy(q_in.at[:, wide_cols(core)], qb.at[core], local_sem.at[2]),
        pltpu.make_async_copy(o_in.at[:, wide_cols(core)], ob.at[core], local_sem.at[3]),
        pltpu.make_async_copy(seg_in, segw.at[3 + core], local_sem.at[4]),
    )

    barrier = pltpu.get_barrier_semaphore()

    def greet(p):
        pl.semaphore_signal(barrier, inc=1, device_id=place(p), device_id_type=MESH)

    greet(partner)

    @pl.when(has_next)
    def _():
        greet(2 * pair + 2)
        greet(2 * pair + 3)

    @pl.when(has_prev)
    def _():
        greet(2 * pair - 2)
        greet(2 * pair - 1)

    @pl.when(has_next2)
    def _():
        greet(2 * pair + 4)
        greet(2 * pair + 5)

    @pl.when(has_prev2)
    def _():
        greet(2 * pair - 3)

    for copy in own:
        copy.start()

    @pl.when(jnp.logical_not(has_prev2))
    def _():
        kv[0] = jnp.zeros((2, TOK, 2 * HEAD), jnp.bfloat16)
        segw[0] = jnp.full((1, TOK), -1, jnp.int32)

    @pl.when(jnp.logical_not(has_prev))
    def _():
        kv[1:3] = jnp.zeros((2, 2, TOK, 2 * HEAD), jnp.bfloat16)
        segw[1:3] = jnp.full((2, 1, TOK), -1, jnp.int32)

    @pl.when(jnp.logical_not(has_next))
    def _():
        back[:, 0:2] = jnp.zeros((2, 2, 2, TOK, HEAD), jnp.bfloat16)

    @pl.when(jnp.logical_not(has_next2))
    def _():
        back[:, 2:4] = jnp.zeros((2, 2, 2, TOK, HEAD), jnp.bfloat16)

    signals = (
        1 + 2 * has_next.astype(jnp.int32) + 2 * has_prev.astype(jnp.int32)
        + 2 * has_next2.astype(jnp.int32) + has_prev2.astype(jnp.int32)
    )
    pl.semaphore_wait(barrier, signals)

    def remote(src, dst, send, recv, p):
        return pltpu.make_async_remote_copy(src, dst, send, recv, place(p), MESH)

    def guarded(cond, fn):
        if cond is None:
            fn()
        else:
            pl.when(cond)(fn)

    targets = [
        (0, 2 * pair + 2, has_next, 1 + core, 0),
        (1, 2 * pair + 3, has_next, 1 + core, 1),
        (2, 2 * pair + 4, has_next2, 0, 0),
        (3, 2 * pair + 5, has_next2, 0, 1),
        (4, partner, None, 3 + core, other),
    ]

    def seg_copy(target):
        n, p, _, slot, _ = target
        return remote(seg_in, segw.at[slot], seg_send.at[n], seg_recv.at[slot], p)

    def send_near(gl):
        def start():
            for _, p, _, slot, two in targets[:2]:
                for i, ref in ((0, k_in), (1, v_in)):
                    remote(
                        ref.at[:, kv_cols(2 * two + gl)], kv.at[slot, i, :, gl * HEAD : (gl + 1) * HEAD],
                        near_send, near_recv.at[gl], p,
                    ).start()
        guarded(has_next, start)

    def send_far(gl):
        def start():
            for _, p, _, slot, two in targets[2:4]:
                for i, ref in ((0, k_in), (1, v_in)):
                    remote(
                        ref.at[:, kv_cols(2 * two + gl)], kv.at[slot, i, :, gl * HEAD : (gl + 1) * HEAD],
                        far_send, far_recv.at[gl], p,
                    ).start()
        guarded(has_next2, start)

    def send_side():
        for i, ref in ((0, k_in), (1, v_in)):
            remote(ref.at[:, both_cols(other)], kv.at[3 + core, i], side_send, side_recv, partner).start()
        remote(q_in.at[:, wide_cols(other)], qb.at[core], q_send.at[0], q_recv.at[0], partner).start()
        remote(o_in.at[:, wide_cols(other)], ob.at[core], q_send.at[1], q_recv.at[1], partner).start()

    send_near(0)
    for target in targets:
        def start_seg(target=target):
            seg_copy(target).start()
        guarded(target[2], start_seg)
    send_side()

    def landed(ref, sem):
        remote(ref, ref, sem, sem, partner).wait_recv()

    def left(ref, sem):
        remote(ref, ref, sem, sem, partner).wait_send()

    def wait_near(gl):
        guarded(has_prev, lambda: landed(kv.at[1:3, :, :, gl * HEAD : (gl + 1) * HEAD], near_recv.at[gl]))

    def wait_far(gl):
        guarded(has_prev2, lambda: landed(kv.at[0, :, :, gl * HEAD : (gl + 1) * HEAD], far_recv.at[gl]))

    def wait_side():
        for copy in own[:4]:
            copy.wait()
        landed(kv.at[3 + other], side_recv)
        landed(qb.at[other], q_recv.at[0])
        landed(ob.at[other], q_recv.at[1])

    own[4].wait()
    landed(segw.at[3 + other], seg_recv.at[3 + other])

    def seg_near():
        landed(segw.at[1], seg_recv.at[1])
        landed(segw.at[2], seg_recv.at[2])
    guarded(has_prev, seg_near)
    guarded(has_prev2, lambda: landed(segw.at[0], seg_recv.at[0]))
    row = lax.broadcasted_iota(jnp.int32, (TOK, TOK), 0)
    col = lax.broadcasted_iota(jnp.int32, (TOK, TOK), 1)
    key_seg = [
        jnp.broadcast_to(segw[slot, 0:1, :].astype(jnp.float32), (TOK, TOK)).T for slot in range(SLOTS)
    ]
    for t in range(2):
        query_seg = segw[3 + t, 0:1, :].astype(jnp.float32)
        merged = jnp.where(row > col, key_seg[t], key_seg[t + 3])
        for b, seg in enumerate((merged, key_seg[t + 1], key_seg[t + 2])):
            bias[t, b] = jnp.where(seg == query_seg, 0.0, -1e30)

    def stacked(block):
        heads = block.shape[1] // HEAD
        return jnp.concatenate([block[:, i * HEAD : (i + 1) * HEAD] for i in range(heads)], 0)

    def dq_local(gl, t):
        cols = q_cols(2 * core + gl)
        return pltpu.make_async_copy(dqs.at[gl, t], dq_out.at[:, cols], dq_sem.at[gl, 0])

    def dq_remote(gl, t):
        cols = q_cols(2 * core + gl)
        return pltpu.make_async_remote_copy(
            dqs.at[gl, t], dq_out.at[:, cols], dq_sem.at[gl, 1], dq_recv.at[gl], place(partner), MESH
        )

    def unit(gl, t, first, after, last=None):
        lanes = slice(gl * HEAD, (gl + 1) * HEAD)
        keys = kv[t : t + 4, 0, :, lanes].reshape(4 * TOK, HEAD)
        vals = kv[t : t + 4, 1, :, lanes].reshape(4 * TOK, HEAD)
        keys_t = keys.astype(jnp.float32).T.astype(jnp.bfloat16)
        mask = bias[t].reshape(3 * TOK, TOK)
        mask = jnp.concatenate([mask, mask], 1)
        upper = jnp.concatenate([row > col, row > col], 1)
        kept = upper.astype(jnp.float32).astype(jnp.bfloat16)
        rest = jnp.logical_not(upper).astype(jnp.float32).astype(jnp.bfloat16)
        pairs_of_heads = GROUP // 2

        def columns(hp):
            return slice((gl * GROUP + hp * 2) * HEAD, (gl * GROUP + hp * 2 + 2) * HEAD)

        def merge(x):
            return jnp.concatenate([jnp.where(upper, x[:TOK], x[3 * TOK :]), x[TOK : 3 * TOK]], 0)

        def spread(x):
            return jnp.concatenate([x[:TOK] * kept, x[TOK:], x[:TOK] * rest], 0)

        def front(hp):
            q = stacked(qb[t, :, columns(hp)])
            o = stacked(ob[t, :, columns(hp)])
            s = merge(lax.dot_general(keys, q, NT, preferred_element_type=jnp.float32)) * INV_ROOT + mask
            dp = merge(lax.dot_general(vals, o, NT, preferred_element_type=jnp.float32))
            return s, dp

        def middle(s, dp):
            top = jnp.max(s, axis=0, keepdims=True)
            w = jnp.exp(s - top)
            scale = 1.0 / jnp.sum(w, axis=0, keepdims=True)
            delta = jnp.sum(w * dp, axis=0, keepdims=True) * scale
            probs = w * scale
            ds = (probs * (dp - delta)).astype(jnp.bfloat16)
            return spread(probs.astype(jnp.bfloat16)), spread(ds)

        def rear(hp, probs, ds, sums, rows):
            q = stacked(qb[t, :, columns(hp)])
            o = stacked(ob[t, :, columns(hp)])
            dk = jnp.dot(ds[rows], q, preferred_element_type=jnp.float32)
            dv = jnp.dot(probs[rows], o, preferred_element_type=jnp.float32)
            if sums is not None:
                dk, dv = sums[0] + dk, sums[1] + dv
            return dk, dv

        def settle(sums, lower):
            count = sums[0].shape[0] // TOK
            dk = (sums[0] * INV_ROOT).reshape(count, TOK, HEAD)
            dv = sums[1].reshape(count, TOK, HEAD)
            for b in range(count):
                slot = t + lower + b
                if first or slot == 0 or slot == 4:
                    acc[gl, slot, 0] = dk[b]
                    acc[gl, slot, 1] = dv[b]
                else:
                    acc[gl, slot, 0] += dk[b]
                    acc[gl, slot, 1] += dv[b]

        def query_side(hp, ds):
            dq = (jnp.dot(keys_t, ds, preferred_element_type=jnp.float32) * INV_ROOT).T
            dqs[gl, t, :, hp * 2 * HEAD : (hp + 1) * 2 * HEAD] = jnp.concatenate([dq[:TOK], dq[TOK:]], 1).astype(jnp.bfloat16)

        ready = front(0)
        done = []
        sums = None
        split = last is not None
        early = slice(0, 2 * TOK) if split else slice(0, 4 * TOK)
        late = slice(2 * TOK, 4 * TOK)
        for hp in range(pairs_of_heads):
            following = front(hp + 1) if hp + 1 < pairs_of_heads else None
            done.append(middle(*ready))
            if hp > 0:
                sums = rear(hp - 1, *done[hp - 1], sums, early)
                if not split:
                    query_side(hp - 1, done[hp - 1][1])
            ready = following
        sums = rear(pairs_of_heads - 1, *done[-1], sums, early)
        settle(sums, 0)
        after()
        if split:
            sums = None
            for hp in range(pairs_of_heads):
                sums = rear(hp, *done[hp], sums, late)
                query_side(hp, done[hp][1])
            settle(sums, 2)
            last()
        else:
            query_side(pairs_of_heads - 1, done[-1][1])
        pl.when(core == t)(lambda: dq_local(gl, t).start())
        pl.when(core != t)(lambda: dq_remote(gl, t).start())

    homes = [
        (0, 2 * pair - 3, has_prev2, 0, 2 + core),
        (1, 2 * pair - 2, has_prev, 1, core),
        (2, 2 * pair - 1, has_prev, 2, core),
        (3, partner, None, 3 + other, 4),
    ]

    def back_copy(home, gl):
        n, p, _, slot, spot = home
        return remote(stage.at[gl, n], back.at[gl, spot], back_send.at[gl, n], back_recv.at[gl, spot // 2], p)

    def send_back(gl, numbers):
        for n in numbers:
            home = homes[n]
            stage[gl, n] = acc[gl, home[3]].astype(jnp.bfloat16)
        for n in numbers:
            home = homes[n]

            def start(home=home):
                back_copy(home, gl).start()
            guarded(home[2], start)

    wait_side()
    wait_near(0)
    send_far(0)
    send_near(1)
    unit(0, 1, True, lambda: None)
    send_far(1)
    wait_far(0)
    unit(0, 0, False, lambda: send_back(0, (0, 1, 2, 3)))
    wait_near(1)
    wait_far(1)
    unit(1, 0, True, lambda: send_back(1, (0,)))
    unit(1, 1, False, lambda: send_back(1, (1, 2)), lambda: send_back(1, (3,)))

    for target in targets:
        def sent(target=target):
            seg_copy(target).wait_send()
        guarded(target[2], sent)
    guarded(has_next, lambda: left(kv.at[0:2], near_send))
    guarded(has_next2, lambda: left(kv.at[0:2], far_send))
    left(kv.at[0], side_send)
    left(qb.at[0], q_send.at[0])
    left(ob.at[0], q_send.at[1])
    dq_local(0, 0).wait()
    dq_local(1, 0).wait()

    for gl in range(2):
        def near(gl=gl):
            landed(back.at[gl, 0:2], back_recv.at[gl, 0])
        guarded(has_next, near)

        def far(gl=gl):
            landed(back.at[gl, 2:4], back_recv.at[gl, 1])
        guarded(has_next2, far)
        landed(back.at[gl, 4], back_recv.at[gl, 2])
        for i, out in ((0, dk_out), (1, dv_out)):
            mine = acc[gl, 3 + core, i]
            mine += back[gl, core, i].astype(jnp.float32)
            mine += back[gl, 2 + core, i].astype(jnp.float32)
            out[:, kv_cols(2 * core + gl)] = mine.astype(jnp.bfloat16)
            theirs = back[gl, 4, i].astype(jnp.float32)
            theirs += back[gl, other, i].astype(jnp.float32)
            theirs += back[gl, 2 + other, i].astype(jnp.float32)
            out[:, kv_cols(2 * other + gl)] = theirs.astype(jnp.bfloat16)

    for gl in range(2):
        for home in homes:
            def returned(home=home, gl=gl):
                back_copy(home, gl).wait_send()
            guarded(home[2], returned)
        dq_remote(gl, 0).wait_send()
        landed(dq_out.at[:, q_cols(2 * other + gl)], dq_recv.at[gl])


def finish(dq, dk, dv, dq_out, dk_out, dv_out, dq_hold, kv_hold, in_sem, out_sem):
    rows = TOK // 4
    trips = []
    for i, (ref, out) in enumerate(((dk, dk_out), (dv, dv_out))):
        trips.append((ref, kv_hold.at[i], out))
    for i in range(4):
        part = pl.ds(i * rows, rows)
        trips.append((dq.at[part], dq_hold.at[part], dq_out.at[part]))
    inward = [pltpu.make_async_copy(ref, hold, in_sem.at[i]) for i, (ref, hold, _) in enumerate(trips)]
    outward = [pltpu.make_async_copy(hold, out, out_sem.at[i]) for i, (_, hold, out) in enumerate(trips)]
    for copy in inward:
        copy.start()
    for first, second in zip(inward, outward):
        first.wait()
        second.start()
    for copy in outward:
        copy.wait()


def body(count, inner, query_rows, key_rows, value_matrix, out_grad, segments):
    bf16, f32 = jnp.bfloat16, jnp.float32
    dma = pltpu.SemaphoreType.DMA
    hbm = pl.BlockSpec(memory_space=pltpu.HBM)
    vmem = pl.BlockSpec(memory_space=pltpu.VMEM)
    parts = pl.pallas_call(
        functools.partial(kernel, inner, count),
        out_shape=(
            jax.ShapeDtypeStruct(query_rows.shape, bf16),
            jax.ShapeDtypeStruct(key_rows.shape, bf16),
            jax.ShapeDtypeStruct(value_matrix.shape, bf16),
        ),
        in_specs=[hbm] * 5,
        out_specs=(hbm, vmem, vmem),
        scratch_shapes=[
            pltpu.VMEM((2, TOK, 2 * WIDE), bf16),
            pltpu.VMEM((2, TOK, 2 * WIDE), bf16),
            pltpu.VMEM((SLOTS, 2, TOK, 2 * HEAD), bf16),
            pltpu.VMEM((SLOTS, 1, TOK), jnp.int32),
            pltpu.VMEM((2, 3, TOK, TOK), f32),
            pltpu.VMEM((2, 2, TOK, WIDE), bf16),
            pltpu.VMEM((2, SLOTS, 2, TOK, HEAD), f32),
            pltpu.VMEM((2, 4, 2, TOK, HEAD), bf16),
            pltpu.VMEM((2, 5, 2, TOK, HEAD), bf16),
            dma((5,)),
            dma((5,)),
            dma((SLOTS,)),
            dma,
            dma((2,)),
            dma,
            dma((2,)),
            dma,
            dma,
            dma((2,)),
            dma((2,)),
            dma((2, 2)),
            dma((2,)),
            dma((2, 4)),
            dma((2, 3)),
        ],
        compiler_params=pltpu.CompilerParams(
            collective_id=0, has_side_effects=True, vmem_limit_bytes=63 * 1024 * 1024
        ),
        cost_estimate=pl.CostEstimate(flops=2_700_000_000, bytes_accessed=4_000_000, transcendentals=2_097_152),
    )(query_rows, key_rows, value_matrix, out_grad, segments.reshape(1, TOK))
    return pl.pallas_call(
        finish,
        out_shape=tuple(jax.ShapeDtypeStruct(part.shape, bf16) for part in parts),
        in_specs=[hbm] * 3,
        out_specs=(hbm,) * 3,
        scratch_shapes=[
            pltpu.VMEM(query_rows.shape, bf16),
            pltpu.VMEM((2,) + key_rows.shape, bf16),
            dma((6,)),
            dma((6,)),
        ],
        compiler_params=pltpu.CompilerParams(vmem_limit_bytes=63 * 1024 * 1024),
    )(*parts)


def solution(mesh):
    count, inner = mesh.size, mesh.shape["fsdp"]
    rows = P(("ctx", "fsdp"), None)
    return jax.shard_map(
        functools.partial(body, count, inner),
        mesh=mesh,
        in_specs=(rows, rows, rows, rows, P(("ctx", "fsdp"))),
        out_specs=(rows, rows, rows),
        check_vma=False,
    )
```

```python
import functools
import math

import jax
import jax.numpy as jnp
from jax import lax
from jax.experimental import pallas as pl
from jax.experimental.pallas import tpu as pltpu
from jax.sharding import PartitionSpec as P

HEAD = 128
GROUP = 8
TOK = 128
SLOTS = 5
WIDE = GROUP * HEAD
INV_ROOT = 1.0 / math.sqrt(HEAD)
MESH = pl.DeviceIdType.MESH
NT = (((1,), (1,)), ((), ()))


def kernel(
    inner, count,
    q_in, k_in, v_in, o_in, seg_in,
    dq_out, dk_out, dv_out,
    qb, ob, kv, segw, bias, dqs, acc, stage, back,
    local_sem, seg_send, seg_recv, near_send, near_recv, far_send, far_recv, side_send, side_recv,
    q_send, q_recv, dq_sem, dq_recv, back_send, back_recv,
):
    pos = lax.axis_index("ctx") * inner + lax.axis_index("fsdp")
    pairs = count // 2
    pair, core = pos // 2, pos % 2
    other = 1 - core

    def place(p):
        return (p // inner, p % inner)

    partner = 2 * pair + other
    has_next = pair + 1 < pairs
    has_next2 = jnp.logical_and(core == 1, pair + 2 < pairs)
    has_prev = pair >= 1
    has_prev2 = pair >= 2

    def kv_cols(h):
        return pl.ds(pl.multiple_of(h * HEAD, HEAD), HEAD)

    def q_cols(h):
        return pl.ds(pl.multiple_of(h * WIDE, WIDE), WIDE)

    def both_cols(p):
        return pl.ds(pl.multiple_of(p * 2 * HEAD, 2 * HEAD), 2 * HEAD)

    def wide_cols(p):
        return pl.ds(pl.multiple_of(p * 2 * WIDE, 2 * WIDE), 2 * WIDE)

    own = (
        pltpu.make_async_copy(k_in.at[:, both_cols(core)], kv.at[3 + core, 0], local_sem.at[0]),
        pltpu.make_async_copy(v_in.at[:, both_cols(core)], kv.at[3 + core, 1], local_sem.at[1]),
        pltpu.make_async_copy(q_in.at[:, wide_cols(core)], qb.at[core], local_sem.at[2]),
        pltpu.make_async_copy(o_in.at[:, wide_cols(core)], ob.at[core], local_sem.at[3]),
        pltpu.make_async_copy(seg_in, segw.at[3 + core], local_sem.at[4]),
    )

    barrier = pltpu.get_barrier_semaphore()

    def greet(p):
        pl.semaphore_signal(barrier, inc=1, device_id=place(p), device_id_type=MESH)

    greet(partner)

    @pl.when(has_next)
    def _():
        greet(2 * pair + 2)
        greet(2 * pair + 3)

    @pl.when(has_prev)
    def _():
        greet(2 * pair - 2)
        greet(2 * pair - 1)

    @pl.when(has_next2)
    def _():
        greet(2 * pair + 4)
        greet(2 * pair + 5)

    @pl.when(has_prev2)
    def _():
        greet(2 * pair - 3)

    for copy in own:
        copy.start()

    @pl.when(jnp.logical_not(has_prev2))
    def _():
        kv[0] = jnp.zeros((2, TOK, 2 * HEAD), jnp.bfloat16)
        segw[0] = jnp.full((1, TOK), -1, jnp.int32)

    @pl.when(jnp.logical_not(has_prev))
    def _():
        kv[1:3] = jnp.zeros((2, 2, TOK, 2 * HEAD), jnp.bfloat16)
        segw[1:3] = jnp.full((2, 1, TOK), -1, jnp.int32)

    @pl.when(jnp.logical_not(has_next))
    def _():
        back[:, 0:2] = jnp.zeros((2, 2, 2, TOK, HEAD), jnp.bfloat16)

    @pl.when(jnp.logical_not(has_next2))
    def _():
        back[:, 2:4] = jnp.zeros((2, 2, 2, TOK, HEAD), jnp.bfloat16)

    signals = (
        1 + 2 * has_next.astype(jnp.int32) + 2 * has_prev.astype(jnp.int32)
        + 2 * has_next2.astype(jnp.int32) + has_prev2.astype(jnp.int32)
    )
    pl.semaphore_wait(barrier, signals)

    def remote(src, dst, send, recv, p):
        return pltpu.make_async_remote_copy(src, dst, send, recv, place(p), MESH)

    def guarded(cond, fn):
        if cond is None:
            fn()
        else:
            pl.when(cond)(fn)

    targets = [
        (0, 2 * pair + 2, has_next, 1 + core, 0),
        (1, 2 * pair + 3, has_next, 1 + core, 1),
        (2, 2 * pair + 4, has_next2, 0, 0),
        (3, 2 * pair + 5, has_next2, 0, 1),
        (4, partner, None, 3 + core, other),
    ]

    def seg_copy(target):
        n, p, _, slot, _ = target
        return remote(seg_in, segw.at[slot], seg_send.at[n], seg_recv.at[slot], p)

    def send_near(gl):
        def start():
            for _, p, _, slot, two in targets[:2]:
                for i, ref in ((0, k_in), (1, v_in)):
                    remote(
                        ref.at[:, kv_cols(2 * two + gl)], kv.at[slot, i, :, gl * HEAD : (gl + 1) * HEAD],
                        near_send, near_recv.at[gl], p,
                    ).start()
        guarded(has_next, start)

    def send_far(gl):
        def start():
            for _, p, _, slot, two in targets[2:4]:
                for i, ref in ((0, k_in), (1, v_in)):
                    remote(
                        ref.at[:, kv_cols(2 * two + gl)], kv.at[slot, i, :, gl * HEAD : (gl + 1) * HEAD],
                        far_send, far_recv.at[gl], p,
                    ).start()
        guarded(has_next2, start)

    def send_side():
        for i, ref in ((0, k_in), (1, v_in)):
            remote(ref.at[:, both_cols(other)], kv.at[3 + core, i], side_send, side_recv, partner).start()
        remote(q_in.at[:, wide_cols(other)], qb.at[core], q_send.at[0], q_recv.at[0], partner).start()
        remote(o_in.at[:, wide_cols(other)], ob.at[core], q_send.at[1], q_recv.at[1], partner).start()

    send_near(0)
    for target in targets:
        def start_seg(target=target):
            seg_copy(target).start()
        guarded(target[2], start_seg)
    send_side()

    def landed(ref, sem):
        remote(ref, ref, sem, sem, partner).wait_recv()

    def left(ref, sem):
        remote(ref, ref, sem, sem, partner).wait_send()

    def wait_near(gl):
        guarded(has_prev, lambda: landed(kv.at[1:3, :, :, gl * HEAD : (gl + 1) * HEAD], near_recv.at[gl]))

    def wait_far(gl):
        guarded(has_prev2, lambda: landed(kv.at[0, :, :, gl * HEAD : (gl + 1) * HEAD], far_recv.at[gl]))

    def wait_side():
        for copy in own[:4]:
            copy.wait()
        landed(kv.at[3 + other], side_recv)
        landed(qb.at[other], q_recv.at[0])
        landed(ob.at[other], q_recv.at[1])

    own[4].wait()
    landed(segw.at[3 + other], seg_recv.at[3 + other])

    def seg_near():
        landed(segw.at[1], seg_recv.at[1])
        landed(segw.at[2], seg_recv.at[2])
    guarded(has_prev, seg_near)
    guarded(has_prev2, lambda: landed(segw.at[0], seg_recv.at[0]))
    row = lax.broadcasted_iota(jnp.int32, (TOK, TOK), 0)
    col = lax.broadcasted_iota(jnp.int32, (TOK, TOK), 1)
    key_seg = [
        jnp.broadcast_to(segw[slot, 0:1, :].astype(jnp.float32), (TOK, TOK)).T for slot in range(SLOTS)
    ]
    for t in range(2):
        query_seg = segw[3 + t, 0:1, :].astype(jnp.float32)
        merged = jnp.where(row > col, key_seg[t], key_seg[t + 3])
        for b, seg in enumerate((merged, key_seg[t + 1], key_seg[t + 2])):
            bias[t, b] = jnp.where(seg == query_seg, 0.0, -1e30)

    def stacked(block):
        heads = block.shape[1] // HEAD
        return jnp.concatenate([block[:, i * HEAD : (i + 1) * HEAD] for i in range(heads)], 0)

    def dq_local(gl, t):
        cols = q_cols(2 * core + gl)
        return pltpu.make_async_copy(dqs.at[gl, t], dq_out.at[:, cols], dq_sem.at[gl, 0])

    def dq_remote(gl, t):
        cols = q_cols(2 * core + gl)
        return pltpu.make_async_remote_copy(
            dqs.at[gl, t], dq_out.at[:, cols], dq_sem.at[gl, 1], dq_recv.at[gl], place(partner), MESH
        )

    def unit(gl, t, first, after, last=None):
        lanes = slice(gl * HEAD, (gl + 1) * HEAD)
        keys = kv[t : t + 4, 0, :, lanes].reshape(4 * TOK, HEAD)
        vals = kv[t : t + 4, 1, :, lanes].reshape(4 * TOK, HEAD)
        keys_t = keys.astype(jnp.float32).T.astype(jnp.bfloat16)
        mask = bias[t].reshape(3 * TOK, TOK)
        mask = jnp.concatenate([mask, mask], 1)
        upper = jnp.concatenate([row > col, row > col], 1)
        kept = upper.astype(jnp.float32).astype(jnp.bfloat16)
        rest = jnp.logical_not(upper).astype(jnp.float32).astype(jnp.bfloat16)
        pairs_of_heads = GROUP // 2

        def columns(hp):
            return slice((gl * GROUP + hp * 2) * HEAD, (gl * GROUP + hp * 2 + 2) * HEAD)

        def merge(x):
            return jnp.concatenate([jnp.where(upper, x[:TOK], x[3 * TOK :]), x[TOK : 3 * TOK]], 0)

        def spread(x):
            return jnp.concatenate([x[:TOK] * kept, x[TOK:], x[:TOK] * rest], 0)

        def front(hp):
            q = stacked(qb[t, :, columns(hp)])
            o = stacked(ob[t, :, columns(hp)])
            s = merge(lax.dot_general(keys, q, NT, preferred_element_type=jnp.float32)) * INV_ROOT + mask
            dp = merge(lax.dot_general(vals, o, NT, preferred_element_type=jnp.float32))
            return s, dp

        def middle(s, dp):
            top = jnp.max(s, axis=0, keepdims=True)
            w = jnp.exp(s - top)
            scale = 1.0 / jnp.sum(w, axis=0, keepdims=True)
            delta = jnp.sum(w * dp, axis=0, keepdims=True) * scale
            probs = w * scale
            ds = (probs * (dp - delta)).astype(jnp.bfloat16)
            return spread(probs.astype(jnp.bfloat16)), spread(ds)

        def rear(hp, probs, ds, sums, rows):
            q = stacked(qb[t, :, columns(hp)])
            o = stacked(ob[t, :, columns(hp)])
            dk = jnp.dot(ds[rows], q, preferred_element_type=jnp.float32)
            dv = jnp.dot(probs[rows], o, preferred_element_type=jnp.float32)
            if sums is not None:
                dk, dv = sums[0] + dk, sums[1] + dv
            return dk, dv

        def settle(sums, lower):
            count = sums[0].shape[0] // TOK
            dk = (sums[0] * INV_ROOT).reshape(count, TOK, HEAD)
            dv = sums[1].reshape(count, TOK, HEAD)
            for b in range(count):
                slot = t + lower + b
                if first or slot == 0 or slot == 4:
                    acc[gl, slot, 0] = dk[b]
                    acc[gl, slot, 1] = dv[b]
                else:
                    acc[gl, slot, 0] += dk[b]
                    acc[gl, slot, 1] += dv[b]

        def query_side(hp, ds):
            dq = (jnp.dot(keys_t, ds, preferred_element_type=jnp.float32) * INV_ROOT).T
            dqs[gl, t, :, hp * 2 * HEAD : (hp + 1) * 2 * HEAD] = jnp.concatenate([dq[:TOK], dq[TOK:]], 1).astype(jnp.bfloat16)

        ready = front(0)
        done = []
        sums = None
        split = last is not None
        early = slice(0, 2 * TOK) if split else slice(0, 4 * TOK)
        late = slice(2 * TOK, 4 * TOK)
        for hp in range(pairs_of_heads):
            following = front(hp + 1) if hp + 1 < pairs_of_heads else None
            done.append(middle(*ready))
            if hp > 0:
                sums = rear(hp - 1, *done[hp - 1], sums, early)
                if not split:
                    query_side(hp - 1, done[hp - 1][1])
            ready = following
        sums = rear(pairs_of_heads - 1, *done[-1], sums, early)
        settle(sums, 0)
        after()
        if split:
            sums = None
            for hp in range(pairs_of_heads):
                sums = rear(hp, *done[hp], sums, late)
                query_side(hp, done[hp][1])
            settle(sums, 2)
            last()
        else:
            query_side(pairs_of_heads - 1, done[-1][1])
        pl.when(core == t)(lambda: dq_local(gl, t).start())
        pl.when(core != t)(lambda: dq_remote(gl, t).start())

    homes = [
        (0, 2 * pair - 3, has_prev2, 0, 2 + core),
        (1, 2 * pair - 2, has_prev, 1, core),
        (2, 2 * pair - 1, has_prev, 2, core),
        (3, partner, None, 3 + other, 4),
    ]

    def back_copy(home, gl):
        n, p, _, slot, spot = home
        return remote(stage.at[gl, n], back.at[gl, spot], back_send.at[gl, n], back_recv.at[gl, spot // 2], p)

    def send_back(gl, numbers):
        for n in numbers:
            home = homes[n]
            stage[gl, n] = acc[gl, home[3]].astype(jnp.bfloat16)
        for n in numbers:
            home = homes[n]

            def start(home=home):
                back_copy(home, gl).start()
            guarded(home[2], start)

    wait_side()
    wait_near(0)
    send_far(0)
    unit(0, 1, True, lambda: None)
    send_near(1)
    send_far(1)
    wait_far(0)
    unit(0, 0, False, lambda: send_back(0, (0, 1, 2, 3)))
    wait_near(1)
    wait_far(1)
    unit(1, 0, True, lambda: send_back(1, (0,)))
    unit(1, 1, False, lambda: send_back(1, (1, 2)), lambda: send_back(1, (3,)))

    for target in targets:
        def sent(target=target):
            seg_copy(target).wait_send()
        guarded(target[2], sent)
    guarded(has_next, lambda: left(kv.at[0:2], near_send))
    guarded(has_next2, lambda: left(kv.at[0:2], far_send))
    left(kv.at[0], side_send)
    left(qb.at[0], q_send.at[0])
    left(ob.at[0], q_send.at[1])
    dq_local(0, 0).wait()
    dq_local(1, 0).wait()

    for gl in range(2):
        def near(gl=gl):
            landed(back.at[gl, 0:2], back_recv.at[gl, 0])
        guarded(has_next, near)

        def far(gl=gl):
            landed(back.at[gl, 2:4], back_recv.at[gl, 1])
        guarded(has_next2, far)
        landed(back.at[gl, 4], back_recv.at[gl, 2])
        for i, out in ((0, dk_out), (1, dv_out)):
            mine = acc[gl, 3 + core, i]
            mine += back[gl, core, i].astype(jnp.float32)
            mine += back[gl, 2 + core, i].astype(jnp.float32)
            out[:, kv_cols(2 * core + gl)] = mine.astype(jnp.bfloat16)
            theirs = back[gl, 4, i].astype(jnp.float32)
            theirs += back[gl, other, i].astype(jnp.float32)
            theirs += back[gl, 2 + other, i].astype(jnp.float32)
            out[:, kv_cols(2 * other + gl)] = theirs.astype(jnp.bfloat16)

    for gl in range(2):
        for home in homes:
            def returned(home=home, gl=gl):
                back_copy(home, gl).wait_send()
            guarded(home[2], returned)
        dq_remote(gl, 0).wait_send()
        landed(dq_out.at[:, q_cols(2 * other + gl)], dq_recv.at[gl])


def finish(dq, dk, dv, dq_out, dk_out, dv_out, dq_hold, kv_hold, in_sem, out_sem):
    rows = TOK // 4
    trips = []
    for i, (ref, out) in enumerate(((dk, dk_out), (dv, dv_out))):
        trips.append((ref, kv_hold.at[i], out))
    for i in range(4):
        part = pl.ds(i * rows, rows)
        trips.append((dq.at[part], dq_hold.at[part], dq_out.at[part]))
    inward = [pltpu.make_async_copy(ref, hold, in_sem.at[i]) for i, (ref, hold, _) in enumerate(trips)]
    outward = [pltpu.make_async_copy(hold, out, out_sem.at[i]) for i, (_, hold, out) in enumerate(trips)]
    for copy in inward:
        copy.start()
    for first, second in zip(inward, outward):
        first.wait()
        second.start()
    for copy in outward:
        copy.wait()


def body(count, inner, query_rows, key_rows, value_matrix, out_grad, segments):
    bf16, f32 = jnp.bfloat16, jnp.float32
    dma = pltpu.SemaphoreType.DMA
    hbm = pl.BlockSpec(memory_space=pltpu.HBM)
    vmem = pl.BlockSpec(memory_space=pltpu.VMEM)
    parts = pl.pallas_call(
        functools.partial(kernel, inner, count),
        out_shape=(
            jax.ShapeDtypeStruct(query_rows.shape, bf16),
            jax.ShapeDtypeStruct(key_rows.shape, bf16),
            jax.ShapeDtypeStruct(value_matrix.shape, bf16),
        ),
        in_specs=[hbm] * 5,
        out_specs=(hbm, vmem, vmem),
        scratch_shapes=[
            pltpu.VMEM((2, TOK, 2 * WIDE), bf16),
            pltpu.VMEM((2, TOK, 2 * WIDE), bf16),
            pltpu.VMEM((SLOTS, 2, TOK, 2 * HEAD), bf16),
            pltpu.VMEM((SLOTS, 1, TOK), jnp.int32),
            pltpu.VMEM((2, 3, TOK, TOK), f32),
            pltpu.VMEM((2, 2, TOK, WIDE), bf16),
            pltpu.VMEM((2, SLOTS, 2, TOK, HEAD), f32),
            pltpu.VMEM((2, 4, 2, TOK, HEAD), bf16),
            pltpu.VMEM((2, 5, 2, TOK, HEAD), bf16),
            dma((5,)),
            dma((5,)),
            dma((SLOTS,)),
            dma,
            dma((2,)),
            dma,
            dma((2,)),
            dma,
            dma,
            dma((2,)),
            dma((2,)),
            dma((2, 2)),
            dma((2,)),
            dma((2, 4)),
            dma((2, 3)),
        ],
        compiler_params=pltpu.CompilerParams(
            collective_id=0, has_side_effects=True, vmem_limit_bytes=63 * 1024 * 1024
        ),
        cost_estimate=pl.CostEstimate(flops=2_700_000_000, bytes_accessed=4_000_000, transcendentals=2_097_152),
    )(query_rows, key_rows, value_matrix, out_grad, segments.reshape(1, TOK))
    return pl.pallas_call(
        finish,
        out_shape=tuple(jax.ShapeDtypeStruct(part.shape, bf16) for part in parts),
        in_specs=[hbm] * 3,
        out_specs=(hbm,) * 3,
        scratch_shapes=[
            pltpu.VMEM(query_rows.shape, bf16),
            pltpu.VMEM((2,) + key_rows.shape, bf16),
            dma((6,)),
            dma((6,)),
        ],
        compiler_params=pltpu.CompilerParams(vmem_limit_bytes=63 * 1024 * 1024),
    )(*parts)


def solution(mesh):
    count, inner = mesh.size, mesh.shape["fsdp"]
    rows = P(("ctx", "fsdp"), None)
    return jax.shard_map(
        functools.partial(body, count, inner),
        mesh=mesh,
        in_specs=(rows, rows, rows, rows, P(("ctx", "fsdp"))),
        out_specs=(rows, rows, rows),
        check_vma=False,
    )
```
